256 devices in a mesh: dom: 64 (over x, z, core), feat: 4 (over y).
Axes of the slice: x: 4, y: 4, z: 8, core: 2. Of those that a mesh axis runs over, the one named last changes fastest.
Arguments:
- features: bfloat16 [262144, 128], P('dom', 'feat'), may hold values from -6 to 6
- weight_one: bfloat16 [128, 256], replicated, may hold values from -0.5 to 0.5
- weight_two: bfloat16 [256, 172], replicated, may hold values from -0.375 to 0.375
- grad_logits: bfloat16 [262144, 172], P('dom', 'feat'), may hold values from -0.15625 to 0.15625
- send_idx: int32 [4096, 64], P('dom'), may hold values from 0 to 4095
- send_count: int32 [4096], P('dom'), may hold values from 16 to 64, as said below
- tile_cols: int32 [2048, 10], P('dom'), may hold values from 0 to 63, as said below
- tile_vals: bfloat16 [2048, 10, 128, 128], P('dom'), may hold values from 0 to 0.06982422
Outputs:
- logits: bfloat16 [262144, 172], P('dom', 'feat')
- grad_one: float32 [128, 256], replicated
- grad_two: float32 [256, 172], replicated
The draws below stay inside these ranges and needn't reach their ends.
Inputs may be any that keep to these rules, and one draw needn't show every extreme that they name: `send_count`: some partition receives 64 live rows from every partition. `tile_cols`: tiles below 32 are a partition's own rows, the others its boundary panel; each row tile lists its own diagonal tile first, and every tile of the boundary panel is listed by some row tile of the partition; tiles may repeat.
All inputs are finite; a program needn't handle non-finite values.
Results may differ from the reference program's by a relative error of at most 0.005.
Values may be sent and summed in bfloat16 or wider, within the bound.
No kernel may reach another device: no remote copies, remote signals or barrier semaphores. Data moves between devices by JAX's collectives and lax.ppermute only.
A program may use at most 128 MiB of HBM per device.

```python
import jax
import jax.numpy as jnp
from jax import lax

F = 128
H = 256
K = 172
R_DEV = 4096
B = 64
TILE = 128
KL = 6
RT = 32
RTR = 32
KR = 4
KT = 10
NODES = 262144
N_DOM = 64


def draw_send_count(key, part):
    key = jax.random.fold_in(key, 11)
    key_counts, key_target = jax.random.split(key)
    counts = jax.random.randint(key_counts, (N_DOM, N_DOM), max(1, B // 4), B + 1)
    target = jax.random.randint(key_target, (), 0, N_DOM)
    counts = jnp.where(jnp.arange(N_DOM)[None, :] == target, B, counts)
    return counts.reshape(N_DOM * N_DOM).astype(jnp.int32)


def draw_tile_cols(key, part):
    key = jax.random.fold_in(key, 23)
    key_local, key_shift = jax.random.split(key)
    row_tiles = jnp.arange(RT, dtype=jnp.int32)
    diagonal = jnp.broadcast_to(row_tiles[None, :, None], (N_DOM, RT, 1))
    others = jax.random.randint(key_local, (N_DOM, RT, KL - 1), 0, RT)
    shifts = jax.random.randint(key_shift, (N_DOM, 1, 1), 0, RTR)
    remote = RT + (row_tiles[None, :, None] * KR + jnp.arange(KR, dtype=jnp.int32)[None, None, :] + shifts) % RTR
    joined = jnp.concatenate([diagonal, others.astype(jnp.int32), remote.astype(jnp.int32)], axis=2)
    return joined.reshape(N_DOM * RT, KT).astype(jnp.int32)


def plant(array, rng, smallest, high):
    spot = [jax.random.randint(jax.random.fold_in(rng, axis), (), 0, length) for axis, length in enumerate(array.shape)]
    widest = array.shape.index(max(array.shape))
    neighbour = spot[:widest] + [(spot[widest] + 1) % array.shape[widest]] + spot[widest + 1:]
    return array.at[tuple(spot)].set(smallest).at[tuple(neighbour)].set(high)


def block_scale(stream_key, shape, cuts, smallest, top_value):
    factor_of = 1.0
    for axis_at, blocks in cuts:
        steps = jax.random.uniform(jax.random.fold_in(jax.random.fold_in(stream_key, 6), axis_at), (blocks,), jnp.float32, smallest / len(cuts), top_value / len(cuts))
        factor_of = factor_of * jnp.repeat(jnp.exp(steps), shape[axis_at] // blocks).reshape((-1,) + (1,) * (len(shape) - 1 - axis_at))
    return factor_of


def scatter_about(key, dims, scale, bound, cuts=(), held_as=jnp.bfloat16):
    drawn = scale * jax.random.normal(key, dims, jnp.float32)
    if cuts:
        drawn = drawn * block_scale(key, dims, cuts, -0.22, 0.18)
    return jnp.clip(drawn, -bound, bound).astype(held_as)


def setup_inputs(seed: int = 0) -> dict:
    key_list = jax.random.split(jax.random.key(seed), 9)
    return {
        "features": scatter_about(key_list[0], (NODES, F), 1.0, 6.0, ((0, 64), (1, 4))),
        "weight_one": scatter_about(key_list[1], (F, H), F ** -0.5, 0.5),
        "weight_two": scatter_about(key_list[2], (H, K), H ** -0.5, 0.375),
        "grad_logits": scatter_about(key_list[3], (NODES, K), 0.01, 0.15625, ((0, 64), (1, 4))),
        "send_idx": plant(jax.random.randint(key_list[4], (N_DOM * N_DOM, B), 0, R_DEV), jax.random.fold_in(key_list[4], 1), 0, R_DEV - 1).astype(jnp.int32),
        "send_count": draw_send_count(jax.random.fold_in(key_list[8], 71), 0),
        "tile_cols": draw_tile_cols(jax.random.fold_in(key_list[8], 71), 0),
        "tile_vals": jnp.clip(0.06982422 * jax.random.uniform(key_list[7], (N_DOM * RT, KT, TILE, TILE), jnp.float32) ** block_scale(key_list[7], (N_DOM * RT, KT, TILE, TILE), ((0, 64),), -0.2, 0.2), 0.0, 0.06982422).astype(jnp.bfloat16),
    }


def boundary_panels(panel_in, send_idx, send_count):
    row_ids = send_idx.reshape(N_DOM, N_DOM, B) + (jnp.arange(N_DOM, dtype=jnp.int32) * R_DEV)[:, None, None]
    live_slots = jnp.arange(B, dtype=jnp.int32)[None, None, :] < send_count.reshape(N_DOM, N_DOM)[:, :, None]
    boundary = jnp.where(live_slots[..., None], panel_in[row_ids], jnp.zeros((), panel_in.dtype))
    return jnp.swapaxes(boundary, 0, 1)

def aggregate(panel_in, send_idx, send_count, tile_cols, tile_vals):
    panel_cols = panel_in.shape[1]
    incoming = boundary_panels(panel_in, send_idx, send_count)
    own_rows = panel_in.reshape(N_DOM, R_DEV, panel_cols)
    tile_index = tile_cols.reshape(N_DOM, RT, KT)
    tile_data = tile_vals.reshape(N_DOM, RT, KT, TILE, TILE)

    def per_part(inputs):
        own_part, incoming_part, index_part, data_part = inputs
        extended = jnp.concatenate([own_part, incoming_part.reshape(N_DOM * B, panel_cols)], axis=0)
        extended = extended.reshape(-1, TILE, panel_cols)
        picked = extended[index_part]
        result = jnp.einsum('tkij,tkjc->tic', data_part.astype(jnp.float32), picked.astype(jnp.float32))
        return result.reshape(R_DEV, panel_cols)
    result = lax.map(per_part, (own_rows, incoming, tile_index, tile_data))
    return result.reshape(NODES, panel_cols)

def reference(features, weight_one, weight_two, grad_logits, send_idx, send_count, tile_cols, tile_vals):

    def apply_graph(panel_in):
        return aggregate(panel_in, send_idx, send_count, tile_cols, tile_vals)
    mixed_one = apply_graph(features.astype(jnp.float32)).astype(jnp.bfloat16)
    pre_one = jnp.dot(mixed_one, weight_one, preferred_element_type=jnp.float32)
    hidden_one = jax.nn.silu(pre_one).astype(jnp.bfloat16)
    mixed_two = apply_graph(hidden_one.astype(jnp.float32)).astype(jnp.bfloat16)
    logits = jnp.dot(mixed_two, weight_two, preferred_element_type=jnp.float32).astype(jnp.bfloat16)
    grad_two = jnp.dot(mixed_two.T, grad_logits, preferred_element_type=jnp.float32)
    grad_mixed = jnp.dot(grad_logits, weight_two.T, preferred_element_type=jnp.float32).astype(jnp.bfloat16)
    unused, pullback = jax.vjp(apply_graph, hidden_one.astype(jnp.float32))
    grad_hidden = pullback(grad_mixed.astype(jnp.float32))[0]
    sigmoid_z = jax.nn.sigmoid(pre_one)
    grad_pre = (grad_hidden * sigmoid_z * (1.0 + pre_one * (1.0 - sigmoid_z))).astype(jnp.bfloat16)
    grad_one = jnp.dot(mixed_one.T, grad_pre, preferred_element_type=jnp.float32)
    return (logits, grad_one, grad_two)
```

```python
import functools

import jax
import jax.numpy as jnp
from jax import lax
from jax.experimental import pallas as pl
from jax.experimental.pallas import tpu as pltpu
from jax.sharding import PartitionSpec as P

BF = jnp.bfloat16
F32 = jnp.float32
VMEM = pltpu.VMEM
LIMIT = 48 * 1024 * 1024
NT = (((1,), (1,)), ((), ()))
NN = (((1,), (0,)), ((), ()))


def dot(a, b, dims=NN):
    return lax.dot_general(a, b, dims, preferred_element_type=F32)


def params():
    return pltpu.CompilerParams(vmem_limit_bytes=LIMIT)


def cost(flops, nbytes):
    return pl.CostEstimate(flops=flops, bytes_accessed=nbytes, transcendentals=0)


def whole():
    return pl.BlockSpec(memory_space=VMEM)


def gather_packed(stack_ref, idx_ref, out_ref, cols):
    chunks = stack_ref.shape[0] // cols
    lanes = stack_ref.shape[1]
    row_ids = lax.broadcasted_iota(jnp.int32, (lanes, 256), 0)
    low = lax.broadcasted_iota(jnp.int32, (16, 128), 1) < 64

    def step(j, carry):
        idx = idx_ref[pl.ds(j, 1), :]
        hot = (row_ids == (idx & (lanes - 1))).astype(BF)
        part = idx >> (lanes.bit_length() - 1)
        got = jnp.zeros((cols, 256), F32)
        for base in range(0, chunks, 4):
            wide = dot(stack_ref[base * cols : (base + 4) * cols, :], hot)
            for c in range(4):
                got = jnp.where(part == base + c, wide[c * cols : (c + 1) * cols], got)
        for pair in range(2):
            top = got[:16, pair * 128 : (pair + 1) * 128]
            bottom = got[16:, pair * 128 : (pair + 1) * 128]
            first = jnp.where(low, top, pltpu.roll(bottom, 64, 1))
            second = jnp.where(low, pltpu.roll(top, 64, 1), bottom)
            out_ref[j * 4 + pair * 2] = first.astype(BF)
            out_ref[j * 4 + pair * 2 + 1] = second.astype(BF)
        return carry

    lax.fori_loop(0, idx_ref.shape[0], step, 0)


def unpack_pair(first, second):
    low = lax.broadcasted_iota(jnp.int32, (16, 128), 1) < 64
    first, second = first.astype(F32), second.astype(F32)
    top = jnp.where(low, first, pltpu.roll(second, 64, 1))
    bottom = jnp.where(low, pltpu.roll(first, 64, 1), second)
    return jnp.concatenate([top, bottom], axis=0).astype(BF)


def fill_stack(stack_ref, panel_ref):
    cols, rows = panel_ref.shape
    for c in range(rows // 256):
        stack_ref[c * cols : (c + 1) * cols, :] = panel_ref[:, c * 256 : (c + 1) * 256]


def gather_kernel(panel_ref, idx_ref, out_ref, stack_ref):
    fill_stack(stack_ref, panel_ref)
    gather_packed(stack_ref, idx_ref, out_ref, panel_ref.shape[0])


def gather_call(panel, idx):
    cols, rows = panel.shape
    pieces = idx.size // 64
    return pl.pallas_call(
        gather_kernel,
        out_shape=jax.ShapeDtypeStruct((pieces, 16, 128), BF),
        in_specs=[whole(), whole()],
        out_specs=whole(),
        scratch_shapes=[VMEM((rows // 256 * cols, 256), BF)],
        compiler_params=params(),
        cost_estimate=cost(2 * 512 * 256 * 4096, 1 << 20),
        name="gather_rows",
    )(panel, idx)


STEP = 4


def transpose_agg_kernel(cols_ref, me_ref, grad_ref, vals_ref, o0, o1, o2, o3, acc):
    step = pl.program_id(0)
    tiles = vals_ref.shape[1]

    @pl.when(step == 0)
    def _():
        acc[...] = jnp.zeros_like(acc)

    for r in range(STEP):
        t = step * STEP + r
        slab = grad_ref[:, r * 128 : (r + 1) * 128]
        side = jnp.concatenate([vals_ref[r, k] for k in range(tiles)], axis=1)
        part = dot(slab, side)
        for k in range(tiles):
            acc[cols_ref[t, k]] += part[:, k * 128 : (k + 1) * 128]

    @pl.when(step == pl.num_programs(0) - 1)
    def _():
        me = me_ref[0]
        for d, out in enumerate((o0, o1, o2, o3)):
            chunk = (me ^ d) * 8
            for j in range(8):
                out[:, j * 128 : (j + 1) * 128] = acc[chunk + j].astype(BF)
                out[:, (8 + j) * 128 : (9 + j) * 128] = acc[32 + chunk + j].astype(BF)


def transpose_agg_call(grad, cols, vals, me):
    width, rows = grad.shape
    row_tiles, tiles = cols.shape
    out = jax.ShapeDtypeStruct((width, 2048), BF)
    return pl.pallas_call(
        transpose_agg_kernel,
        out_shape=(out,) * 4,
        grid_spec=pltpu.PrefetchScalarGridSpec(
            num_scalar_prefetch=2,
            grid=(row_tiles // STEP,),
            in_specs=[
                pl.BlockSpec((width, STEP * 128), lambda s, *_: (0, s)),
                pl.BlockSpec((STEP, tiles, 128, 128), lambda s, *_: (s, 0, 0, 0)),
            ],
            out_specs=[pl.BlockSpec((width, 2048), lambda s, *_: (0, 0))] * 4,
            scratch_shapes=[VMEM((64, width, 128), F32)],
        ),
        compiler_params=params(),
        cost_estimate=cost(2 * 48 * 128 * 128 * 320 * 4, 11 << 20),
        name="agg_transposed",
    )(cols, me, grad, vals)


def agg_rows(step, cols_ref, ext, vals_ref, r):
    tiles = vals_ref.shape[1]
    t = step * STEP + r
    total = None
    for k in range(0, tiles, 2):
        left = jnp.concatenate([ext[cols_ref[t, k]], ext[cols_ref[t, k + 1]]], axis=1)
        right = jnp.concatenate([vals_ref[r, k], vals_ref[r, k + 1]], axis=1)
        part = dot(left, right, NT)
        total = part if total is None else total + part
    return total


def agg_one_kernel(cols_ref, me_ref, panel_ref, recv_ref, idx_ref, vals_ref, packed_ref, o0, o1, o2, o3, ext, stack):
    step = pl.program_id(0)

    @pl.when(step == 0)
    def _():
        for e in range(32):
            ext[e] = panel_ref[:, e * 128 : (e + 1) * 128]
            ext[32 + e] = unpack_pair(recv_ref[2 * e], recv_ref[2 * e + 1])

    for r in range(STEP):
        total = agg_rows(step, cols_ref, ext, vals_ref, r).astype(BF)
        place = pl.multiple_of((step * STEP + r) // 2 * 32, 32)
        stack[pl.ds(place, 32), (r % 2) * 128 : (r % 2 + 1) * 128] = total

    @pl.when(step == pl.num_programs(0) - 1)
    def _():
        me = me_ref[0]
        for d, out in enumerate((o0, o1, o2, o3)):
            for j in range(4):
                place = pl.multiple_of(((me ^ d) * 4 + j) * 32, 32)
                out[:, j * 256 : (j + 1) * 256] = stack[pl.ds(place, 32), :]
        gather_packed(stack, idx_ref, packed_ref, 32)


def agg_one_call(panel, received, idx, cols, vals, me):
    row_tiles, tiles = cols.shape
    pieces = received.shape[0]
    out = jax.ShapeDtypeStruct((32, 1024), BF)
    return pl.pallas_call(
        agg_one_kernel,
        out_shape=(jax.ShapeDtypeStruct((pieces, 16, 128), BF),) + (out,) * 4,
        grid_spec=pltpu.PrefetchScalarGridSpec(
            num_scalar_prefetch=2,
            grid=(row_tiles // STEP,),
            in_specs=[
                pl.BlockSpec((32, 4096), lambda s, *_: (0, 0)),
                pl.BlockSpec((pieces, 16, 128), lambda s, *_: (0, 0, 0)),
                pl.BlockSpec(idx.shape, lambda s, *_: (0, 0)),
                pl.BlockSpec((STEP, tiles, 128, 128), lambda s, *_: (s, 0, 0, 0)),
            ],
            out_specs=[pl.BlockSpec((pieces, 16, 128), lambda s, *_: (0, 0, 0))]
            + [pl.BlockSpec((32, 1024), lambda s, *_: (0, 0))] * 4,
            scratch_shapes=[VMEM((64, 32, 128), BF), VMEM((512, 256), BF)],
        ),
        compiler_params=params(),
        cost_estimate=cost(2 * 32 * 128 * 128 * 320 * 8, 11 << 20),
        name="agg_one",
    )(cols, me, panel, received, idx, vals)


def dense_kernel(me_ref, *refs):
    own = refs[0:4]
    far = refs[4:8]
    zs = refs[8:12]
    w1t, w2, w2t = refs[12:15]
    ys = refs[15:19]
    gs = refs[19:23]
    mix, zed, hid, gp, yall, gall = refs[23:29]
    me = me_ref[0]
    for d in range(4):
        f = me ^ d
        at = pl.multiple_of(f * 32, 32)
        mix[pl.ds(at, 32), 0:1024] = own[d][...]
        for e in range(8):
            mix[pl.ds(at, 32), 1024 + e * 128 : 1024 + (e + 1) * 128] = unpack_pair(
                far[d][2 * e], far[d][2 * e + 1]
            )
        zed[pl.ds(pl.multiple_of(f * 48, 16), 48), :] = zs[d][...]
    for c in range(8):
        lanes = slice(c * 256, (c + 1) * 256)
        pre = dot(w1t[...], mix[:, lanes])
        gate = 1.0 / (1.0 + jnp.exp(-pre))
        hidden = (pre * gate).astype(BF)
        hid[:, lanes] = hidden
        yall[:, lanes] = dot(w2t[...], hidden).astype(BF)
        gh = dot(w2[...], zed[:, lanes])
        gp[:, lanes] = (gh * gate * (1.0 + pre * (1.0 - gate))).astype(BF)
    p1 = dot(mix[...], gp[...], NT)
    p2 = dot(zed[...], hid[...], NT)
    gall[0:128] = p1[:, :128]
    gall[128:256] = p1[:, 128:]
    gall[256:448] = p2[:, :128]
    gall[448:640] = p2[:, 128:]
    for d in range(4):
        f = me ^ d
        ys[d][...] = yall[pl.ds(pl.multiple_of(f * 48, 16), 48), :]
        gs[d][...] = gall[pl.ds(pl.multiple_of(f * 160, 8), 160), :]


def dense_call(me, own, far, zs, w1t, w2, w2t):
    return pl.pallas_call(
        dense_kernel,
        out_shape=(jax.ShapeDtypeStruct((48, 2048), BF),) * 4
        + (jax.ShapeDtypeStruct((160, 128), F32),) * 4,
        in_specs=[pl.BlockSpec(memory_space=pltpu.SMEM)] + [whole()] * 15,
        out_specs=[whole()] * 8,
        scratch_shapes=[
            VMEM((128, 2048), BF),
            VMEM((192, 2048), BF),
            VMEM((256, 2048), BF),
            VMEM((256, 2048), BF),
            VMEM((192, 2048), BF),
            VMEM((640, 128), F32),
        ],
        compiler_params=params(),
        cost_estimate=cost(2 * 2048 * 256 * 1500, 4 << 20),
        name="dense",
    )(me, *own, *far, *zs, w1t, w2, w2t)


def agg_two_kernel(cols_ref, me_ref, y0, y1, y2, y3, vals_ref, out_ref, ext):
    step = pl.program_id(0)

    @pl.when(step == 0)
    def _():
        me = me_ref[0]
        for d, y in enumerate((y0, y1, y2, y3)):
            chunk = (me ^ d) * 8
            for j in range(8):
                ext[chunk + j] = y[:, j * 128 : (j + 1) * 128]
                ext[32 + chunk + j] = y[:, (8 + j) * 128 : (9 + j) * 128]

    for r in range(STEP):
        total = agg_rows(step, cols_ref, ext, vals_ref, r).astype(BF)
        out_ref[:, r * 128 : (r + 1) * 128] = total[: out_ref.shape[0]]


def agg_two_call(ys, cols, vals, me, classes):
    row_tiles, tiles = cols.shape
    return pl.pallas_call(
        agg_two_kernel,
        out_shape=jax.ShapeDtypeStruct((classes, row_tiles * 128), BF),
        grid_spec=pltpu.PrefetchScalarGridSpec(
            num_scalar_prefetch=2,
            grid=(row_tiles // STEP,),
            in_specs=[pl.BlockSpec((48, 2048), lambda s, *_: (0, 0))] * 4
            + [pl.BlockSpec((STEP, tiles, 128, 128), lambda s, *_: (s, 0, 0, 0))],
            out_specs=pl.BlockSpec((classes, STEP * 128), lambda s, *_: (0, s)),
            scratch_shapes=[VMEM((64, 48, 128), BF)],
        ),
        compiler_params=params(),
        cost_estimate=cost(2 * 48 * 128 * 128 * 320 * 4, 11 << 20),
        name="agg_two",
    )(cols, me, *ys, vals)


def finish_kernel(me_ref, g0, g1, g2, g3, one_ref, two_ref, buf):
    me = me_ref[0]
    for d, g in enumerate((g0, g1, g2, g3)):
        buf[pl.ds(pl.multiple_of((me ^ d) * 160, 8), 160), :] = g[...]
    one_ref[:, :128] = buf[0:128]
    one_ref[:, 128:] = buf[128:256]
    per = two_ref.shape[0] // 4
    for f in range(4):
        two_ref[f * per : (f + 1) * per, :128] = buf[256 + 48 * f : 256 + 48 * f + per]
        two_ref[f * per : (f + 1) * per, 128:] = buf[448 + 48 * f : 448 + 48 * f + per]


def finish_call(me, gs, classes):
    return pl.pallas_call(
        finish_kernel,
        out_shape=(
            jax.ShapeDtypeStruct((128, 256), F32),
            jax.ShapeDtypeStruct((classes, 256), F32),
        ),
        in_specs=[pl.BlockSpec(memory_space=pltpu.SMEM)] + [whole()] * 4,
        out_specs=[whole()] * 2,
        scratch_shapes=[VMEM((640, 128), F32)],
        compiler_params=params(),
        name="finish",
    )(me, *gs)


def swap(x, axis, size, mask):
    return lax.ppermute(x, axis, [(i, i ^ mask) for i in range(size)])


def on_device(
    features, weight_one, weight_two, grad_logits, send_idx, send_count, tile_cols, tile_vals
):
    partitions = lax.axis_size("dom")
    feat = lax.axis_size("feat")
    me = lax.axis_index("feat").astype(jnp.int32)
    me_arr = me.reshape(1)
    bound_rows = send_idx.shape[1]
    class_cols = grad_logits.shape[1]
    hidden = weight_one.shape[1]

    def swap_feat(x, d):
        return swap(x, "feat", feat, d)

    def swap_dom(x, mask):
        return swap(x, "dom", partitions, mask)

    live = jnp.arange(bound_rows, dtype=jnp.int32)[None, :] < send_count[:, None]
    idx = jnp.where(live, send_idx, -1).reshape(-1, 256)
    panel = features.T
    grad = jnp.pad(grad_logits.T, ((0, 48 - class_cols), (0, 0)))
    w2 = jnp.pad(weight_two.reshape(hidden, feat, class_cols), ((0, 0), (0, 0), (0, 48 - class_cols)))
    w2 = w2.reshape(hidden, feat * 48)
    w1t = weight_one.T
    w2t = w2.T

    packed_one = gather_call(panel, idx)
    received_one = lax.all_to_all(packed_one, "dom", split_axis=0, concat_axis=0, tiled=True)
    zs = transpose_agg_call(grad, tile_cols, tile_vals, me_arr)
    zs = [zs[0]] + [swap_feat(zs[d], d) for d in (1, 2, 3)]
    packed_two, *mixed = agg_one_call(panel, received_one, idx, tile_cols, tile_vals, me_arr)
    own = [mixed[0]] + [swap_feat(mixed[d], d) for d in (1, 2, 3)]
    received_two = lax.all_to_all(packed_two, "dom", split_axis=0, concat_axis=0, tiled=True)
    pieces = partitions // feat

    def far_block(d):
        return lax.dynamic_slice_in_dim(received_two, (me ^ d) * pieces, pieces, 0)

    far = [far_block(0)] + [swap_feat(far_block(d), d) for d in (1, 2, 3)]
    outs = dense_call(me_arr, own, far, zs, w1t, w2, w2t)
    ys, gs = outs[:4], outs[4:]
    gs_in = [swap_feat(gs[d], d) for d in (1, 2, 3)]
    ys = [ys[0]] + [swap_feat(ys[d], d) for d in (1, 2, 3)]
    total = (gs[0] + gs_in[0]) + (gs_in[1] + gs_in[2])
    total = total + swap_dom(total, 1)
    near = [swap_dom(total, 16 * d) for d in (1, 2, 3)]
    total = (total + near[0]) + (near[1] + near[2])
    for mask in (2, 4, 8):
        total = total + swap_dom(total, mask)
    parts = [total] + [swap_feat(total, d) for d in (1, 2, 3)]
    grad_one, grad_two = finish_call(me_arr, parts, feat * class_cols)
    logits = agg_two_call(ys, tile_cols, tile_vals, me_arr, class_cols)
    return (logits.T, grad_one, grad_two.T)


def solution(mesh):
    return jax.shard_map(
        on_device,
        mesh=mesh,
        in_specs=(
            P("dom", "feat"),
            P(),
            P(),
            P("dom", "feat"),
            P("dom", None),
            P("dom"),
            P("dom", None),
            P("dom", None, None, None),
        ),
        out_specs=(P("dom", "feat"), P(), P()),
        check_vma=False,
    )
```

```python
import functools

import jax
import jax.numpy as jnp
from jax import lax
from jax.experimental import pallas as pl
from jax.experimental.pallas import tpu as pltpu
from jax.sharding import PartitionSpec as P

BF = jnp.bfloat16
F32 = jnp.float32
VMEM = pltpu.VMEM
LIMIT = 24 * 1024 * 1024
LARGE = 48 * 1024 * 1024
NT = (((1,), (1,)), ((), ()))
NN = (((1,), (0,)), ((), ()))


def dot(a, b, dims=NN):
    return lax.dot_general(a, b, dims, preferred_element_type=F32)


def params(limit=LIMIT):
    return pltpu.CompilerParams(vmem_limit_bytes=limit)


def cost(flops, nbytes):
    return pl.CostEstimate(flops=flops, bytes_accessed=nbytes, transcendentals=0)


def whole():
    return pl.BlockSpec(memory_space=VMEM)


def gather_packed(stack_ref, idx_ref, out_ref, cols):
    chunks = stack_ref.shape[0] // cols
    lanes = stack_ref.shape[1]
    row_ids = lax.broadcasted_iota(jnp.int32, (lanes, 256), 0)
    low = lax.broadcasted_iota(jnp.int32, (16, 128), 1) < 64

    def step(j, carry):
        idx = idx_ref[pl.ds(j, 1), :]
        hot = (row_ids == (idx & (lanes - 1))).astype(BF)
        part = idx >> (lanes.bit_length() - 1)
        got = jnp.zeros((cols, 256), F32)
        wide = dot(stack_ref[...], hot)
        for c in range(chunks):
            got = jnp.where(part == c, wide[c * cols : (c + 1) * cols], got)
        for pair in range(2):
            top = got[:16, pair * 128 : (pair + 1) * 128]
            bottom = got[16:, pair * 128 : (pair + 1) * 128]
            first = jnp.where(low, top, pltpu.roll(bottom, 64, 1))
            second = jnp.where(low, pltpu.roll(top, 64, 1), bottom)
            out_ref[j * 4 + pair * 2] = first.astype(BF)
            out_ref[j * 4 + pair * 2 + 1] = second.astype(BF)
        return carry

    lax.fori_loop(0, idx_ref.shape[0], step, 0, unroll=8)


def unpack_pair(first, second):
    low = lax.broadcasted_iota(jnp.int32, (16, 128), 1) < 64
    first, second = first.astype(F32), second.astype(F32)
    top = jnp.where(low, first, pltpu.roll(second, 64, 1))
    bottom = jnp.where(low, pltpu.roll(first, 64, 1), second)
    return jnp.concatenate([top, bottom], axis=0).astype(BF)


def fill_stack(stack_ref, panel_ref):
    cols, rows = panel_ref.shape
    for c in range(rows // 256):
        stack_ref[c * cols : (c + 1) * cols, :] = panel_ref[:, c * 256 : (c + 1) * 256]


def gather_kernel(panel_ref, idx_ref, out_ref, stack_ref):
    fill_stack(stack_ref, panel_ref)
    gather_packed(stack_ref, idx_ref, out_ref, panel_ref.shape[0])


def gather_call(panel, idx):
    cols, rows = panel.shape
    pieces = idx.size // 64
    return pl.pallas_call(
        gather_kernel,
        out_shape=jax.ShapeDtypeStruct((pieces, 16, 128), BF),
        in_specs=[whole(), whole()],
        out_specs=whole(),
        scratch_shapes=[VMEM((rows // 256 * cols, 256), BF)],
        compiler_params=params(),
        cost_estimate=cost(2 * 512 * 256 * 4096, 1 << 20),
        name="gather_rows",
    )(panel, idx)


def smem():
    return pl.BlockSpec(memory_space=pltpu.SMEM)


UNROLL = 8


def anywhere():
    return pl.BlockSpec(memory_space=pl.ANY)


def held_scratch(vals, group):
    return [VMEM(vals.shape, vals.dtype), pltpu.SemaphoreType.DMA((vals.shape[0] // group,))]


def fetch(vals_ref, held, sems, s, group, first=0):
    return pltpu.make_async_copy(
        vals_ref.at[pl.ds(first + s * group, group)], held.at[pl.ds(s * group, group)], sems.at[s]
    )


def transpose_agg_kernel(cols_ref, me_ref, grad_ref, vals_ref, o0, o1, o2, o3, acc, held, sems):
    row_tiles, tiles = vals_ref.shape[:2]
    classes = grad_ref.shape[0]
    for s in range(row_tiles // UNROLL):
        fetch(vals_ref, held, sems, s, UNROLL).start()
    acc[...] = jnp.zeros_like(acc)

    def body(s, carry):
        fetch(vals_ref, held, sems, s, UNROLL).wait()
        for r in range(UNROLL):
            t = s * UNROLL + r
            slab = grad_ref[:, pl.ds(pl.multiple_of(t * 128, 128), 128)]
            side = jnp.concatenate([held[t, k] for k in range(tiles)], axis=1)
            part = dot(slab, side)
            for k in range(tiles):
                acc[cols_ref[k, t], :classes] += part[:, k * 128 : (k + 1) * 128]
        return carry

    lax.fori_loop(0, row_tiles // UNROLL, body, 0)
    me = me_ref[0]
    for d, out in enumerate((o0, o1, o2, o3)):
        chunk = (me ^ d) * 8
        for j in range(8):
            out[:, j * 128 : (j + 1) * 128] = acc[chunk + j].astype(BF)
            out[:, (8 + j) * 128 : (9 + j) * 128] = acc[32 + chunk + j].astype(BF)


def transpose_agg_call(grad, cols, vals, me):
    width = 48
    return pl.pallas_call(
        transpose_agg_kernel,
        out_shape=(jax.ShapeDtypeStruct((width, 2048), BF),) * 4,
        in_specs=[smem(), smem(), whole(), anywhere()],
        out_specs=[whole()] * 4,
        scratch_shapes=[VMEM((64, width, 128), F32)] + held_scratch(vals, UNROLL),
        compiler_params=params(LARGE),
        cost_estimate=cost(2 * 48 * 128 * 128 * 320 * 4, 11 << 20),
        name="agg_transposed",
    )(cols, me, grad, vals)


def agg_tile(t, place, cols_ref, ext, held):
    tiles = held.shape[1]
    left = jnp.concatenate([held[place, k] for k in range(tiles)], axis=1)
    right = jnp.concatenate([ext[cols_ref[k, t]] for k in range(tiles)], axis=1)
    return dot(left, right, NT).T.astype(BF)


def agg_one_kernel(
    cols_ref, me_ref, panel_ref, recv_ref, idx_ref, vals_ref, packed_ref, o0, o1, o2, o3, ext, stack, held, sems
):
    row_tiles = vals_ref.shape[0]
    for s in range(row_tiles // UNROLL):
        fetch(vals_ref, held, sems, s, UNROLL).start()
    for e in range(32):
        ext[e] = panel_ref[:, e * 128 : (e + 1) * 128]
        ext[32 + e] = unpack_pair(recv_ref[2 * e], recv_ref[2 * e + 1])

    def body(s, carry):
        fetch(vals_ref, held, sems, s, UNROLL).wait()
        for r in range(UNROLL):
            place = pl.multiple_of((s * (UNROLL // 2) + r // 2) * 32, 32)
            total = agg_tile(s * UNROLL + r, s * UNROLL + r, cols_ref, ext, held)
            stack[pl.ds(place, 32), (r % 2) * 128 : (r % 2 + 1) * 128] = total
        return carry

    lax.fori_loop(0, row_tiles // UNROLL, body, 0)
    gather_packed(stack, idx_ref, packed_ref, 32)
    me = me_ref[0]
    for d, out in enumerate((o0, o1, o2, o3)):
        for j in range(4):
            place = pl.multiple_of(((me ^ d) * 4 + j) * 32, 32)
            out[:, j * 256 : (j + 1) * 256] = stack[pl.ds(place, 32), :]


def agg_one_call(panel, received, idx, cols, vals, me):
    pieces = received.shape[0]
    out = jax.ShapeDtypeStruct((32, 1024), BF)
    return pl.pallas_call(
        agg_one_kernel,
        out_shape=(jax.ShapeDtypeStruct((pieces, 16, 128), BF),) + (out,) * 4,
        in_specs=[smem(), smem(), whole(), whole(), whole(), anywhere()],
        out_specs=[whole()] * 5,
        scratch_shapes=[VMEM((64, 32, 128), BF), VMEM((512, 256), BF)] + held_scratch(vals, UNROLL),
        compiler_params=params(LARGE),
        cost_estimate=cost(2 * 32 * 128 * 128 * 320 * 8, 11 << 20),
        name="agg_one",
    )(cols, me, panel, received, idx, vals)


def dense_body(mix, zed, w1t, w2, w2t, hid, gp, yall):
    rows = mix.shape[1]
    for c in range(rows // 256):
        lanes = slice(c * 256, (c + 1) * 256)
        pre = dot(w1t[...], mix[:, lanes])
        gate = 1.0 / (1.0 + jnp.exp(-pre))
        hidden = (pre * gate).astype(BF)
        hid[:, lanes] = hidden
        yall[:, lanes] = dot(w2t[...], hidden).astype(BF)
        gh = dot(w2[...], zed[:, lanes])
        gp[:, lanes] = (gh * gate * (1.0 + pre * (1.0 - gate))).astype(BF)
    return dot(mix[...], gp[...], NT), dot(zed[...], hid[...], NT)


def dense_own_kernel(me_ref, *refs):
    own, zs = refs[0:4], refs[4:8]
    w1t, w2, w2t = refs[8:11]
    yall, p1_ref, p2_ref = refs[11:14]
    mix, zed, hid, gp = refs[14:18]
    me = me_ref[0]
    for d in range(4):
        f = me ^ d
        mix[pl.ds(pl.multiple_of(f * 32, 32), 32), :] = own[d][...]
        zed[pl.ds(pl.multiple_of(f * 48, 16), 48), :] = zs[d][:, :1024]
    p1, p2 = dense_body(mix, zed, w1t, w2, w2t, hid, gp, yall)
    p1_ref[...] = p1
    p2_ref[...] = p2


def dense_far_kernel(me_ref, *refs):
    far, zs = refs[0:4], refs[4:8]
    w1t, w2, w2t, y_own, p1_ref, p2_ref = refs[8:14]
    ys, gs = refs[14:18], refs[18:22]
    mix, zed, hid, gp, yall, gall = refs[22:28]
    me = me_ref[0]
    for d in range(4):
        f = me ^ d
        at = pl.multiple_of(f * 32, 32)
        for e in range(8):
            mix[pl.ds(at, 32), e * 128 : (e + 1) * 128] = unpack_pair(far[d][2 * e], far[d][2 * e + 1])
        zed[pl.ds(pl.multiple_of(f * 48, 16), 48), :] = zs[d][:, 1024:]
    p1, p2 = dense_body(mix, zed, w1t, w2, w2t, hid, gp, yall)
    for d in range(4):
        place = pl.ds(pl.multiple_of((me ^ d) * 48, 16), 48)
        ys[d][:, :1024] = y_own[place, :]
        ys[d][:, 1024:] = yall[place, :]
    p1 = p1 + p1_ref[...]
    p2 = p2 + p2_ref[...]
    gall[0:128] = p1[:, :128]
    gall[128:256] = p1[:, 128:]
    gall[256:448] = p2[:, :128]
    gall[448:640] = p2[:, 128:]
    for d in range(4):
        gs[d][...] = gall[pl.ds(pl.multiple_of((me ^ d) * 160, 8), 160), :]


def dense_scratch():
    return [
        VMEM((128, 1024), BF),
        VMEM((192, 1024), BF),
        VMEM((256, 1024), BF),
        VMEM((256, 1024), BF),
    ]


def dense_own_call(me, own, zs, w1t, w2, w2t):
    return pl.pallas_call(
        dense_own_kernel,
        out_shape=(
            jax.ShapeDtypeStruct((192, 1024), BF),
            jax.ShapeDtypeStruct((128, 256), F32),
            jax.ShapeDtypeStruct((192, 256), F32),
        ),
        in_specs=[smem()] + [whole()] * 11,
        out_specs=[whole()] * 3,
        scratch_shapes=dense_scratch(),
        compiler_params=params(),
        cost_estimate=cost(2 * 1024 * 256 * 1500, 4 << 20),
        name="dense_own",
    )(me, *own, *zs, w1t, w2, w2t)


def dense_far_call(me, far, zs, w1t, w2, w2t, y_own, p1, p2):
    return pl.pallas_call(
        dense_far_kernel,
        out_shape=(jax.ShapeDtypeStruct((48, 2048), BF),) * 4
        + (jax.ShapeDtypeStruct((160, 128), F32),) * 4,
        in_specs=[smem()] + [whole()] * 14,
        out_specs=[whole()] * 8,
        scratch_shapes=dense_scratch() + [VMEM((192, 1024), BF), VMEM((640, 128), F32)],
        compiler_params=params(),
        cost_estimate=cost(2 * 1024 * 256 * 1500, 4 << 20),
        name="dense_far",
    )(me, *far, *zs, w1t, w2, w2t, y_own, p1, p2)


def spread_kernel(me_ref, *refs):
    ext = refs[4]
    me = me_ref[0]
    for d in range(4):
        chunk = (me ^ d) * 8
        for j in range(8):
            ext[chunk + j] = refs[d][:, j * 128 : (j + 1) * 128]
            ext[32 + chunk + j] = refs[d][:, (8 + j) * 128 : (9 + j) * 128]


def spread_call(me, ys):
    return pl.pallas_call(
        spread_kernel,
        out_shape=jax.ShapeDtypeStruct((64, 48, 128), BF),
        in_specs=[smem()] + [whole()] * 4,
        out_specs=whole(),
        compiler_params=params(),
        cost_estimate=cost(0, 100 << 20),
        name="spread",
    )(me, *ys)


def agg_two_call(first, count, ext, cols, vals, classes):
    def kernel(cols_ref, ext_ref, vals_ref, out_ref):
        for r in range(count):
            total = agg_tile(first + r, first + r, cols_ref, ext_ref, vals_ref)
            out_ref[:, r * 128 : (r + 1) * 128] = total[:classes]

    return pl.pallas_call(
        kernel,
        out_shape=jax.ShapeDtypeStruct((classes, count * 128), BF),
        in_specs=[smem(), whole(), whole()],
        out_specs=whole(),
        compiler_params=params(),
        cost_estimate=cost(2 * 48 * 128 * 128 * 10 * count * 4, count * 330000),
        name="agg_two",
    )(cols, ext, vals)


def finish_kernel(me_ref, g0, g1, g2, g3, one_ref, two_ref, buf):
    me = me_ref[0]
    for d, g in enumerate((g0, g1, g2, g3)):
        buf[pl.ds(pl.multiple_of((me ^ d) * 160, 8), 160), :] = g[...]
    one_ref[:, :128] = buf[0:128]
    one_ref[:, 128:] = buf[128:256]
    per = two_ref.shape[0] // 4
    for f in range(4):
        two_ref[f * per : (f + 1) * per, :128] = buf[256 + 48 * f : 256 + 48 * f + per]
        two_ref[f * per : (f + 1) * per, 128:] = buf[448 + 48 * f : 448 + 48 * f + per]


def finish_call(me, gs, classes):
    return pl.pallas_call(
        finish_kernel,
        out_shape=(
            jax.ShapeDtypeStruct((128, 256), F32),
            jax.ShapeDtypeStruct((classes, 256), F32),
        ),
        in_specs=[pl.BlockSpec(memory_space=pltpu.SMEM)] + [whole()] * 4,
        out_specs=[whole()] * 2,
        scratch_shapes=[VMEM((640, 128), F32)],
        compiler_params=params(),
        name="finish",
    )(me, *gs)


def swap(x, axis, size, mask):
    return lax.ppermute(x, axis, [(i, i ^ mask) for i in range(size)])


def after(x, *others):
    return lax.optimization_barrier((x, *others))[0]


def swap_sum(blocks, move):
    moved = [move(blocks[d], d) for d in (1, 2, 3)]
    return (blocks[0] + moved[0]) + (moved[1] + moved[2])


def on_device(
    features, weight_one, weight_two, grad_logits, send_idx, send_count, tile_cols, tile_vals
):
    partitions = lax.axis_size("dom")
    feat = lax.axis_size("feat")
    me = lax.axis_index("feat").astype(jnp.int32)
    me_arr = me.reshape(1)
    bound_rows = send_idx.shape[1]
    class_cols = grad_logits.shape[1]
    hidden = weight_one.shape[1]

    def swap_feat(x, d):
        return swap(x, "feat", feat, d)

    def swap_dom(x, mask):
        return swap(x, "dom", partitions, mask)

    live = jnp.arange(bound_rows, dtype=jnp.int32)[None, :] < send_count[:, None]
    idx = jnp.where(live, send_idx, -1).reshape(-1, 256)
    panel = features.T
    grad = grad_logits.T
    cols = tile_cols.T
    w2 = jnp.pad(weight_two.reshape(hidden, feat, class_cols), ((0, 0), (0, 0), (0, 48 - class_cols)))
    w2 = w2.reshape(hidden, feat * 48)
    w1t = weight_one.T
    w2t = w2.T

    packed_one = gather_call(panel, idx)
    received_one = lax.all_to_all(packed_one, "dom", split_axis=0, concat_axis=0, tiled=True)
    zs = transpose_agg_call(grad, cols, tile_vals, me_arr)
    received_one = after(received_one, zs[0])
    zs = [zs[0]] + [swap_feat(zs[d], d) for d in (1, 2, 3)]
    packed_two, *mixed = agg_one_call(panel, received_one, idx, cols, tile_vals, me_arr)
    packed_two = after(packed_two, *zs)
    received_two = lax.all_to_all(packed_two, "dom", split_axis=0, concat_axis=0, tiled=True)
    own = [mixed[0]] + [swap_feat(mixed[d], d) for d in (1, 2, 3)]
    pieces = partitions // feat

    def far_block(d):
        return lax.dynamic_slice_in_dim(received_two, (me ^ d) * pieces, pieces, 0)

    near = far_block(0)
    far = [near] + [swap_feat(far_block(d), d) for d in (1, 2, 3)]
    own[0] = after(own[0], near)
    y_own, p1, p2 = dense_own_call(me_arr, own, zs, w1t, w2, w2t)
    outs = dense_far_call(me_arr, far, zs, w1t, w2, w2t, y_own, p1, p2)
    ys, gs = outs[:4], outs[4:]
    total = swap_sum(gs, swap_feat)
    ys = [ys[0]] + [swap_feat(ys[d], d) for d in (1, 2, 3)]
    total = total + swap_dom(total, 1)
    total = swap_sum([total] * 4, lambda x, d: swap_dom(x, 16 * d))
    ext = spread_call(me_arr, ys)
    out = []
    row_tiles = tile_cols.shape[0]
    cuts = [0, row_tiles // 8, row_tiles * 9 // 16, row_tiles]

    def beside(moved):
        first, last = cuts[len(out) : len(out) + 2]
        out.append(agg_two_call(first, last - first, ext, cols, tile_vals, class_cols))
        *moved, out[-1] = lax.optimization_barrier((*moved, out[-1]))
        return moved

    ext, total = lax.optimization_barrier((ext, total))
    (moved,) = beside([swap_dom(total, 8)])
    total = total + moved
    ext, total = lax.optimization_barrier((ext, total))
    moved = beside([swap_dom(total, d) for d in (2, 4, 6)])
    total = (total + moved[0]) + (moved[1] + moved[2])
    ext, total = lax.optimization_barrier((ext, total))
    moved = beside([swap_feat(total, d) for d in (1, 2, 3)])
    logits = jnp.concatenate(out, axis=1)
    logits, *moved = lax.optimization_barrier((logits, *moved))
    grad_one, grad_two = finish_call(me_arr, [total] + moved, feat * class_cols)
    return (logits.T, grad_one, grad_two.T)


def solution(mesh):
    return jax.shard_map(
        on_device,
        mesh=mesh,
        in_specs=(
            P("dom", "feat"),
            P(),
            P(),
            P("dom", "feat"),
            P("dom", None),
            P("dom"),
            P("dom", None),
            P("dom", None, None, None),
        ),
        out_specs=(P("dom", "feat"), P(), P()),
        check_vma=False,
    )
```

```python
import functools

import jax
import jax.numpy as jnp
from jax import lax
from jax.experimental import pallas as pl
from jax.experimental.pallas import tpu as pltpu
from jax.sharding import PartitionSpec as P

BF = jnp.bfloat16
F32 = jnp.float32
VMEM = pltpu.VMEM
LIMIT = 24 * 1024 * 1024
LARGE = 48 * 1024 * 1024
NT = (((1,), (1,)), ((), ()))
NN = (((1,), (0,)), ((), ()))


def dot(a, b, dims=NN):
    return lax.dot_general(a, b, dims, preferred_element_type=F32)


def params(limit=LIMIT):
    return pltpu.CompilerParams(vmem_limit_bytes=limit)


def cost(flops, nbytes):
    return pl.CostEstimate(flops=flops, bytes_accessed=nbytes, transcendentals=0)


def whole():
    return pl.BlockSpec(memory_space=VMEM)


def gather_packed(stack_ref, idx_ref, out_ref, cols):
    chunks = stack_ref.shape[0] // cols
    lanes = stack_ref.shape[1]
    row_ids = lax.broadcasted_iota(jnp.int32, (lanes, 256), 0)
    low = lax.broadcasted_iota(jnp.int32, (16, 128), 1) < 64

    def step(j, carry):
        idx = idx_ref[pl.ds(j, 1), :]
        hot = (row_ids == (idx & (lanes - 1))).astype(BF)
        part = idx >> (lanes.bit_length() - 1)
        got = jnp.zeros((cols, 256), F32)
        wide = dot(stack_ref[...], hot)
        for c in range(chunks):
            got = jnp.where(part == c, wide[c * cols : (c + 1) * cols], got)
        for pair in range(2):
            top = got[:16, pair * 128 : (pair + 1) * 128]
            bottom = got[16:, pair * 128 : (pair + 1) * 128]
            first = jnp.where(low, top, pltpu.roll(bottom, 64, 1))
            second = jnp.where(low, pltpu.roll(top, 64, 1), bottom)
            out_ref[j * 4 + pair * 2] = first.astype(BF)
            out_ref[j * 4 + pair * 2 + 1] = second.astype(BF)
        return carry

    lax.fori_loop(0, idx_ref.shape[0], step, 0, unroll=8)


def unpack_pair(first, second):
    low = lax.broadcasted_iota(jnp.int32, (16, 128), 1) < 64
    first, second = first.astype(F32), second.astype(F32)
    top = jnp.where(low, first, pltpu.roll(second, 64, 1))
    bottom = jnp.where(low, pltpu.roll(first, 64, 1), second)
    return jnp.concatenate([top, bottom], axis=0).astype(BF)


def gather_kernel(live_ref, panel_ref, send_ref, out_ref, idx_ref, stack_ref, lists, count_ref, sems):
    cols = panel_ref.shape[0]
    lanes = stack_ref.shape[1]
    chunks = panel_ref.shape[1] // lanes
    copies = [
        pltpu.make_async_copy(live_ref, count_ref, sems.at[chunks + 1]),
        pltpu.make_async_copy(send_ref, lists, sems.at[chunks]),
    ] + [
        pltpu.make_async_copy(
            panel_ref.at[:, pl.ds(c * lanes, lanes)], stack_ref.at[pl.ds(c * cols, cols), :], sems.at[c]
        )
        for c in range(chunks)
    ]
    for copy in copies:
        copy.start()
    copies[0].wait()
    copies[1].wait()
    bound = lists.shape[1]
    slot = lax.broadcasted_iota(jnp.int32, (1, bound), 1)
    per = lanes // bound
    for j in range(idx_ref.shape[0]):
        rows = [
            jnp.where(slot < count_ref[q], lists[q : q + 1, :], -1) for q in range(j * per, (j + 1) * per)
        ]
        idx_ref[j : j + 1, :] = jnp.concatenate(rows, axis=1)
    for copy in copies[2:]:
        copy.wait()
    gather_packed(stack_ref, idx_ref, out_ref, cols)


def gather_call(panel, send_idx, send_count):
    cols, rows = panel.shape
    pieces, bound = send_idx.shape
    return pl.pallas_call(
        gather_kernel,
        out_shape=(
            jax.ShapeDtypeStruct((pieces, 16, 128), BF),
            jax.ShapeDtypeStruct((pieces * bound // 256, 256), jnp.int32),
        ),
        in_specs=[anywhere()] * 3,
        out_specs=[whole(), whole()],
        scratch_shapes=[
            VMEM((rows // 256 * cols, 256), BF),
            VMEM((pieces, bound), jnp.int32),
            pltpu.SMEM((pieces,), jnp.int32),
            pltpu.SemaphoreType.DMA((rows // 256 + 2,)),
        ],
        compiler_params=params(60 * 1024 * 1024),
        cost_estimate=cost(2 * 512 * 256 * 4096, 1 << 20),
        name="gather_rows",
    )(send_count, panel, send_idx)


def smem():
    return pl.BlockSpec(memory_space=pltpu.SMEM)


UNROLL = 8


def anywhere():
    return pl.BlockSpec(memory_space=pl.ANY)


def held_scratch(vals, group):
    return [VMEM(vals.shape, vals.dtype), pltpu.SemaphoreType.DMA((vals.shape[0] // group,))]


def fetch(vals_ref, held, sems, s, group, first=0):
    return pltpu.make_async_copy(
        vals_ref.at[pl.ds(first + s * group, group)], held.at[pl.ds(s * group, group)], sems.at[s]
    )


def transpose_agg_kernel(cols_ref, me_ref, grad_ref, vals_ref, o0, o1, o2, o3, acc, held, sems):
    row_tiles, tiles = vals_ref.shape[:2]
    classes = grad_ref.shape[0]
    for s in range(row_tiles // UNROLL):
        fetch(vals_ref, held, sems, s, UNROLL).start()
    acc[...] = jnp.zeros_like(acc)

    def body(s, carry):
        fetch(vals_ref, held, sems, s, UNROLL).wait()
        for r in range(UNROLL):
            t = s * UNROLL + r
            slab = grad_ref[:, pl.ds(pl.multiple_of(t * 128, 128), 128)]
            side = jnp.concatenate([held[t, k] for k in range(tiles)], axis=1)
            part = dot(slab, side)
            for k in range(tiles):
                acc[cols_ref[k, t], :classes] += part[:, k * 128 : (k + 1) * 128]
        return carry

    lax.fori_loop(0, row_tiles // UNROLL, body, 0)
    me = me_ref[0]
    for d, out in enumerate((o0, o1, o2, o3)):
        chunk = (me ^ d) * 8
        for j in range(8):
            out[:, j * 128 : (j + 1) * 128] = acc[chunk + j].astype(BF)
            out[:, (8 + j) * 128 : (9 + j) * 128] = acc[32 + chunk + j].astype(BF)


def transpose_agg_call(grad, cols, vals, me):
    width = 48
    return pl.pallas_call(
        transpose_agg_kernel,
        out_shape=(jax.ShapeDtypeStruct((width, 2048), BF),) * 4,
        in_specs=[smem(), smem(), whole(), anywhere()],
        out_specs=[whole()] * 4,
        scratch_shapes=[VMEM((64, width, 128), F32)] + held_scratch(vals, UNROLL),
        compiler_params=params(LARGE),
        cost_estimate=cost(2 * 48 * 128 * 128 * 320 * 4, 11 << 20),
        name="agg_transposed",
    )(cols, me, grad, vals)


def agg_tile(t, place, cols_ref, ext, held):
    tiles = held.shape[1]
    left = jnp.concatenate([held[place, k] for k in range(tiles)], axis=1)
    right = jnp.concatenate([ext[cols_ref[k, t]] for k in range(tiles)], axis=1)
    return dot(left, right, NT).T.astype(BF)


def agg_one_kernel(
    cols_ref, me_ref, panel_ref, recv_ref, idx_ref, vals_ref, packed_ref, o0, o1, o2, o3, ext, stack, held, sems
):
    row_tiles = vals_ref.shape[0]
    for s in range(row_tiles // UNROLL):
        fetch(vals_ref, held, sems, s, UNROLL).start()
    for e in range(32):
        ext[e] = panel_ref[:, e * 128 : (e + 1) * 128]
        ext[32 + e] = unpack_pair(recv_ref[2 * e], recv_ref[2 * e + 1])

    def body(s, carry):
        fetch(vals_ref, held, sems, s, UNROLL).wait()
        for r in range(UNROLL):
            place = pl.multiple_of((s * (UNROLL // 2) + r // 2) * 32, 32)
            total = agg_tile(s * UNROLL + r, s * UNROLL + r, cols_ref, ext, held)
            stack[pl.ds(place, 32), (r % 2) * 128 : (r % 2 + 1) * 128] = total
        return carry

    lax.fori_loop(0, row_tiles // UNROLL, body, 0)
    gather_packed(stack, idx_ref, packed_ref, 32)
    me = me_ref[0]
    for d, out in enumerate((o0, o1, o2, o3)):
        for j in range(4):
            place = pl.multiple_of(((me ^ d) * 4 + j) * 32, 32)
            out[:, j * 256 : (j + 1) * 256] = stack[pl.ds(place, 32), :]


def agg_one_call(panel, received, idx, cols, vals, me):
    pieces = received.shape[0]
    out = jax.ShapeDtypeStruct((32, 1024), BF)
    return pl.pallas_call(
        agg_one_kernel,
        out_shape=(jax.ShapeDtypeStruct((pieces, 16, 128), BF),) + (out,) * 4,
        in_specs=[smem(), smem(), whole(), whole(), whole(), anywhere()],
        out_specs=[whole()] * 5,
        scratch_shapes=[VMEM((64, 32, 128), BF), VMEM((512, 256), BF)] + held_scratch(vals, UNROLL),
        compiler_params=params(LARGE),
        cost_estimate=cost(2 * 32 * 128 * 128 * 320 * 8, 11 << 20),
        name="agg_one",
    )(cols, me, panel, received, idx, vals)


def dense_body(mix, zed, w1t, w2, w2t, hid, gp, yall):
    rows = mix.shape[1]
    for c in range(rows // 256):
        lanes = slice(c * 256, (c + 1) * 256)
        pre = dot(w1t[...], mix[:, lanes])
        gate = 1.0 / (1.0 + jnp.exp(-pre))
        hidden = (pre * gate).astype(BF)
        hid[:, lanes] = hidden
        yall[:, lanes] = dot(w2t[...], hidden).astype(BF)
        gh = dot(w2[...], zed[:, lanes])
        gp[:, lanes] = (gh * gate * (1.0 + pre * (1.0 - gate))).astype(BF)
    return dot(mix[...], gp[...], NT), dot(zed[...], hid[...], NT)


def dense_own_kernel(me_ref, *refs):
    own, zs = refs[0:4], refs[4:8]
    w1t, w2, w2t = refs[8:11]
    yall, p1_ref, p2_ref = refs[11:14]
    mix, zed, hid, gp = refs[14:18]
    me = me_ref[0]
    for d in range(4):
        f = me ^ d
        mix[pl.ds(pl.multiple_of(f * 32, 32), 32), :] = own[d][...]
        zed[pl.ds(pl.multiple_of(f * 48, 16), 48), :] = zs[d][:, :1024]
    p1, p2 = dense_body(mix, zed, w1t, w2, w2t, hid, gp, yall)
    p1_ref[...] = p1
    p2_ref[...] = p2


def dense_far_kernel(me_ref, *refs):
    far, zs = refs[0:4], refs[4:8]
    w1t, w2, w2t, y_own, p1_ref, p2_ref = refs[8:14]
    ys, gs = refs[14:18], refs[18:22]
    mix, zed, hid, gp, yall, gall = refs[22:28]
    me = me_ref[0]
    for d in range(4):
        f = me ^ d
        at = pl.multiple_of(f * 32, 32)
        for e in range(8):
            mix[pl.ds(at, 32), e * 128 : (e + 1) * 128] = unpack_pair(far[d][2 * e], far[d][2 * e + 1])
        zed[pl.ds(pl.multiple_of(f * 48, 16), 48), :] = zs[d][:, 1024:]
    p1, p2 = dense_body(mix, zed, w1t, w2, w2t, hid, gp, yall)
    for d in range(4):
        place = pl.ds(pl.multiple_of((me ^ d) * 48, 16), 48)
        ys[d][:, :1024] = y_own[place, :]
        ys[d][:, 1024:] = yall[place, :]
    p1 = p1 + p1_ref[...]
    p2 = p2 + p2_ref[...]
    gall[0:128] = p1[:, :128]
    gall[128:256] = p1[:, 128:]
    gall[256:448] = p2[:, :128]
    gall[448:640] = p2[:, 128:]
    for d in range(4):
        gs[d][...] = gall[pl.ds(pl.multiple_of((me ^ d) * 160, 8), 160), :]


def dense_scratch():
    return [
        VMEM((128, 1024), BF),
        VMEM((192, 1024), BF),
        VMEM((256, 1024), BF),
        VMEM((256, 1024), BF),
    ]


def dense_own_call(me, own, zs, w1t, w2, w2t):
    return pl.pallas_call(
        dense_own_kernel,
        out_shape=(
            jax.ShapeDtypeStruct((192, 1024), BF),
            jax.ShapeDtypeStruct((128, 256), F32),
            jax.ShapeDtypeStruct((192, 256), F32),
        ),
        in_specs=[smem()] + [whole()] * 11,
        out_specs=[whole()] * 3,
        scratch_shapes=dense_scratch(),
        compiler_params=params(),
        cost_estimate=cost(2 * 1024 * 256 * 1500, 4 << 20),
        name="dense_own",
    )(me, *own, *zs, w1t, w2, w2t)


def dense_far_call(me, far, zs, w1t, w2, w2t, y_own, p1, p2):
    return pl.pallas_call(
        dense_far_kernel,
        out_shape=(jax.ShapeDtypeStruct((48, 2048), BF),) * 4
        + (jax.ShapeDtypeStruct((160, 128), F32),) * 4,
        in_specs=[smem()] + [whole()] * 14,
        out_specs=[whole()] * 8,
        scratch_shapes=dense_scratch() + [VMEM((192, 1024), BF), VMEM((640, 128), F32)],
        compiler_params=params(),
        cost_estimate=cost(2 * 1024 * 256 * 1500, 4 << 20),
        name="dense_far",
    )(me, *far, *zs, w1t, w2, w2t, y_own, p1, p2)


def spread_kernel(me_ref, *refs):
    ext = refs[4]
    me = me_ref[0]
    for d in range(4):
        chunk = (me ^ d) * 8
        for j in range(8):
            ext[chunk + j] = refs[d][:, j * 128 : (j + 1) * 128]
            ext[32 + chunk + j] = refs[d][:, (8 + j) * 128 : (9 + j) * 128]


def spread_call(me, ys):
    return pl.pallas_call(
        spread_kernel,
        out_shape=jax.ShapeDtypeStruct((64, 48, 128), BF),
        in_specs=[smem()] + [whole()] * 4,
        out_specs=whole(),
        compiler_params=params(),
        cost_estimate=cost(0, 100 << 20),
        name="spread",
    )(me, *ys)


def agg_two_call(first, count, ext, cols, vals, classes, done):
    lead = sum(part.shape[1] for part in done)

    def kernel(cols_ref, ext_ref, vals_ref, *refs):
        out_ref = refs[-1]
        at = 0
        for part in refs[:-1]:
            out_ref[:, at : at + part.shape[1]] = part[...]
            at += part.shape[1]
        for r in range(count):
            total = agg_tile(first + r, first + r, cols_ref, ext_ref, vals_ref)
            out_ref[:, at + r * 128 : at + (r + 1) * 128] = total[:classes]

    return pl.pallas_call(
        kernel,
        out_shape=jax.ShapeDtypeStruct((classes, lead + count * 128), BF),
        in_specs=[smem()] + [whole()] * (2 + len(done)),
        out_specs=whole(),
        compiler_params=params(),
        cost_estimate=cost(2 * 48 * 128 * 128 * 10 * count * 4, count * 330000),
        name="agg_two",
    )(cols, ext, vals, *done)


def finish_kernel(me_ref, g0, g1, g2, g3, one_ref, two_ref, buf):
    me = me_ref[0]
    for d, g in enumerate((g0, g1, g2, g3)):
        buf[pl.ds(pl.multiple_of((me ^ d) * 160, 8), 160), :] = g[...]
    one_ref[:, :128] = buf[0:128]
    one_ref[:, 128:] = buf[128:256]
    per = two_ref.shape[0] // 4
    for f in range(4):
        two_ref[f * per : (f + 1) * per, :128] = buf[256 + 48 * f : 256 + 48 * f + per]
        two_ref[f * per : (f + 1) * per, 128:] = buf[448 + 48 * f : 448 + 48 * f + per]


def finish_call(me, gs, classes):
    return pl.pallas_call(
        finish_kernel,
        out_shape=(
            jax.ShapeDtypeStruct((128, 256), F32),
            jax.ShapeDtypeStruct((classes, 256), F32),
        ),
        in_specs=[pl.BlockSpec(memory_space=pltpu.SMEM)] + [whole()] * 4,
        out_specs=[whole()] * 2,
        scratch_shapes=[VMEM((640, 128), F32)],
        compiler_params=params(),
        name="finish",
    )(me, *gs)


def swap(x, axis, size, mask):
    return lax.ppermute(x, axis, [(i, i ^ mask) for i in range(size)])


def after(x, *others):
    return lax.optimization_barrier((x, *others))[0]


def swap_sum(blocks, move):
    moved = [move(blocks[d], d) for d in (1, 2, 3)]
    return (blocks[0] + moved[0]) + (moved[1] + moved[2])


def on_device(
    features, weight_one, weight_two, grad_logits, send_idx, send_count, tile_cols, tile_vals
):
    partitions = lax.axis_size("dom")
    feat = lax.axis_size("feat")
    me = lax.axis_index("feat").astype(jnp.int32)
    me_arr = me.reshape(1)
    class_cols = grad_logits.shape[1]
    hidden = weight_one.shape[1]

    def swap_feat(x, d):
        return swap(x, "feat", feat, d)

    def swap_dom(x, mask):
        return swap(x, "dom", partitions, mask)

    panel = features.T
    grad = grad_logits.T
    cols = tile_cols.T
    w2 = jnp.pad(weight_two.reshape(hidden, feat, class_cols), ((0, 0), (0, 0), (0, 48 - class_cols)))
    w2 = w2.reshape(hidden, feat * 48)
    w1t = weight_one.T
    w2t = w2.T

    packed_one, idx = gather_call(panel, send_idx, send_count)
    received_one = lax.all_to_all(packed_one, "dom", split_axis=0, concat_axis=0, tiled=True)
    zs = transpose_agg_call(grad, cols, tile_vals, me_arr)
    received_one = after(received_one, zs[0])
    zs = [zs[0]] + [swap_feat(zs[d], d) for d in (1, 2, 3)]
    packed_two, *mixed = agg_one_call(panel, received_one, idx, cols, tile_vals, me_arr)
    packed_two = after(packed_two, zs[1], zs[3])
    received_two = lax.all_to_all(packed_two, "dom", split_axis=0, concat_axis=0, tiled=True)
    own = [mixed[0]] + [swap_feat(mixed[d], d) for d in (1, 2, 3)]
    pieces = partitions // feat

    def far_block(d):
        return lax.dynamic_slice_in_dim(received_two, (me ^ d) * pieces, pieces, 0)

    near = far_block(0)
    far = [near] + [swap_feat(far_block(d), d) for d in (1, 2, 3)]
    own[0] = after(own[0], near)
    y_own, p1, p2 = dense_own_call(me_arr, own, zs, w1t, w2, w2t)
    outs = dense_far_call(me_arr, far, zs, w1t, w2, w2t, y_own, p1, p2)
    ys, gs = outs[:4], outs[4:]
    total = swap_sum(gs, swap_feat)
    ys = [ys[0]] + [swap_feat(ys[d], d) for d in (1, 2, 3)]
    total = total + swap_dom(total, 1)
    total = swap_sum([total] * 4, lambda x, d: swap_dom(x, 16 * d))
    ext = spread_call(me_arr, ys)
    out = []
    row_tiles = tile_cols.shape[0]
    cuts = [0, row_tiles // 8, row_tiles * 9 // 16, row_tiles]

    def beside(moved):
        first, last = cuts[len(out) : len(out) + 2]
        done = out if last == row_tiles else []
        out.append(agg_two_call(first, last - first, ext, cols, tile_vals, class_cols, done))
        *moved, out[-1] = lax.optimization_barrier((*moved, out[-1]))
        return moved

    ext, total = lax.optimization_barrier((ext, total))
    (moved,) = beside([swap_dom(total, 8)])
    total = total + moved
    ext, total = lax.optimization_barrier((ext, total))
    moved = beside([swap_dom(total, d) for d in (2, 4, 6)])
    total = (total + moved[0]) + (moved[1] + moved[2])
    ext, total = lax.optimization_barrier((ext, total))
    moved = beside([swap_feat(total, d) for d in (1, 2, 3)])
    logits = out[-1]
    grad_one, grad_two = finish_call(me_arr, [total] + moved, feat * class_cols)
    return (logits.T, grad_one, grad_two.T)


def solution(mesh):
    return jax.shard_map(
        on_device,
        mesh=mesh,
        in_specs=(
            P("dom", "feat"),
            P(),
            P(),
            P("dom", "feat"),
            P("dom", None),
            P("dom"),
            P("dom", None),
            P("dom", None, None, None),
        ),
        out_specs=(P("dom", "feat"), P(), P()),
        check_vma=False,
    )
```

```python
import functools

import jax
import jax.numpy as jnp
from jax import lax
from jax.experimental import pallas as pl
from jax.experimental.pallas import tpu as pltpu
from jax.sharding import PartitionSpec as P

BF = jnp.bfloat16
F32 = jnp.float32
VMEM = pltpu.VMEM
LIMIT = 24 * 1024 * 1024
LARGE = 48 * 1024 * 1024
PARTNERS = (0, 1, 3, 2)
NT = (((1,), (1,)), ((), ()))
NN = (((1,), (0,)), ((), ()))


def dot(a, b, dims=NN):
    return lax.dot_general(a, b, dims, preferred_element_type=F32)


def params(limit=LIMIT):
    return pltpu.CompilerParams(vmem_limit_bytes=limit)


def cost(flops, nbytes):
    return pl.CostEstimate(flops=flops, bytes_accessed=nbytes, transcendentals=0)


def whole():
    return pl.BlockSpec(memory_space=VMEM)


def gather_packed(stack_ref, idx_ref, out_ref, cols):
    chunks = stack_ref.shape[0] // cols
    lanes = stack_ref.shape[1]
    row_ids = lax.broadcasted_iota(jnp.int32, (lanes, 256), 0)
    low = lax.broadcasted_iota(jnp.int32, (16, 128), 1) < 64

    def step(j, carry):
        idx = idx_ref[pl.ds(j, 1), :]
        hot = (row_ids == (idx & (lanes - 1))).astype(BF)
        part = idx >> (lanes.bit_length() - 1)
        got = jnp.zeros((cols, 256), F32)
        wide = dot(stack_ref[...], hot)
        for c in range(chunks):
            got = jnp.where(part == c, wide[c * cols : (c + 1) * cols], got)
        for pair in range(2):
            top = got[:16, pair * 128 : (pair + 1) * 128]
            bottom = got[16:, pair * 128 : (pair + 1) * 128]
            first = jnp.where(low, top, pltpu.roll(bottom, 64, 1))
            second = jnp.where(low, pltpu.roll(top, 64, 1), bottom)
            out_ref[j * 4 + pair * 2] = first.astype(BF)
            out_ref[j * 4 + pair * 2 + 1] = second.astype(BF)
        return carry

    lax.fori_loop(0, idx_ref.shape[0], step, 0, unroll=8)


def unpack_pair(first, second):
    low = lax.broadcasted_iota(jnp.int32, (16, 128), 1) < 64
    first, second = first.astype(F32), second.astype(F32)
    top = jnp.where(low, first, pltpu.roll(second, 64, 1))
    bottom = jnp.where(low, pltpu.roll(first, 64, 1), second)
    return jnp.concatenate([top, bottom], axis=0).astype(BF)


def gather_kernel(live_ref, panel_ref, send_ref, out_ref, idx_ref, stack_ref, lists, count_ref, sems):
    cols = panel_ref.shape[0]
    lanes = stack_ref.shape[1]
    chunks = panel_ref.shape[1] // lanes
    copies = [
        pltpu.make_async_copy(live_ref, count_ref, sems.at[chunks + 1]),
        pltpu.make_async_copy(send_ref, lists, sems.at[chunks]),
    ] + [
        pltpu.make_async_copy(
            panel_ref.at[:, pl.ds(c * lanes, lanes)], stack_ref.at[pl.ds(c * cols, cols), :], sems.at[c]
        )
        for c in range(chunks)
    ]
    for copy in copies:
        copy.start()
    copies[0].wait()
    copies[1].wait()
    bound = lists.shape[1]
    slot = lax.broadcasted_iota(jnp.int32, (1, bound), 1)
    per = lanes // bound
    for j in range(idx_ref.shape[0]):
        rows = [
            jnp.where(slot < count_ref[q], lists[q : q + 1, :], -1) for q in range(j * per, (j + 1) * per)
        ]
        idx_ref[j : j + 1, :] = jnp.concatenate(rows, axis=1)
    for copy in copies[2:]:
        copy.wait()
    gather_packed(stack_ref, idx_ref, out_ref, cols)


def gather_call(panel, send_idx, send_count):
    cols, rows = panel.shape
    pieces, bound = send_idx.shape
    return pl.pallas_call(
        gather_kernel,
        out_shape=(
            jax.ShapeDtypeStruct((pieces, 16, 128), BF),
            jax.ShapeDtypeStruct((pieces * bound // 256, 256), jnp.int32),
        ),
        in_specs=[anywhere()] * 3,
        out_specs=[whole(), whole()],
        scratch_shapes=[
            VMEM((rows // 256 * cols, 256), BF),
            VMEM((pieces, bound), jnp.int32),
            pltpu.SMEM((pieces,), jnp.int32),
            pltpu.SemaphoreType.DMA((rows // 256 + 2,)),
        ],
        compiler_params=params(60 * 1024 * 1024),
        cost_estimate=cost(2 * 512 * 256 * 4096, 1 << 20),
        name="gather_rows",
    )(send_count, panel, send_idx)


def smem():
    return pl.BlockSpec(memory_space=pltpu.SMEM)


UNROLL = 8


def anywhere():
    return pl.BlockSpec(memory_space=pl.ANY)


def held_scratch(vals, group):
    return [VMEM(vals.shape, vals.dtype), pltpu.SemaphoreType.DMA((vals.shape[0] // group,))]


def list_scratch(cols):
    return [pltpu.SMEM(cols.shape, cols.dtype), pltpu.SemaphoreType.DMA]


def fetch(vals_ref, held, sems, s, group, first=0):
    return pltpu.make_async_copy(
        vals_ref.at[pl.ds(first + s * group, group)], held.at[pl.ds(s * group, group)], sems.at[s]
    )


def transpose_agg_kernel(list_ref, me_ref, grad_ref, vals_ref, o0, o1, o2, o3, acc, cols_ref, col_sem, held, sems):
    row_tiles, tiles = vals_ref.shape[:2]
    classes = grad_ref.shape[0]
    lists = pltpu.make_async_copy(list_ref, cols_ref, col_sem)
    lists.start()
    for s in range(row_tiles // UNROLL):
        fetch(vals_ref, held, sems, s, UNROLL).start()
    acc[...] = jnp.zeros_like(acc)
    lists.wait()

    def body(s, carry):
        fetch(vals_ref, held, sems, s, UNROLL).wait()
        for r in range(UNROLL):
            t = s * UNROLL + r
            slab = grad_ref[:, pl.ds(pl.multiple_of(t * 128, 128), 128)]
            side = jnp.concatenate([held[t, k] for k in range(tiles)], axis=1)
            part = dot(slab, side)
            for k in range(tiles):
                acc[cols_ref[k, t], :classes] += part[:, k * 128 : (k + 1) * 128]
        return carry

    lax.fori_loop(0, row_tiles // UNROLL, body, 0)
    me = me_ref[0]
    for d, out in enumerate((o0, o1, o2, o3)):
        chunk = (me ^ d) * 8
        for j in range(8):
            out[:, j * 128 : (j + 1) * 128] = acc[chunk + j].astype(BF)
            out[:, (8 + j) * 128 : (9 + j) * 128] = acc[32 + chunk + j].astype(BF)


def transpose_agg_call(grad, cols, vals, me):
    width = 48
    return pl.pallas_call(
        transpose_agg_kernel,
        out_shape=(jax.ShapeDtypeStruct((width, 2048), BF),) * 4,
        in_specs=[anywhere(), smem(), whole(), anywhere()],
        out_specs=[whole()] * 4,
        scratch_shapes=[VMEM((64, width, 128), F32)] + list_scratch(cols) + held_scratch(vals, UNROLL),
        compiler_params=params(LARGE),
        cost_estimate=cost(2 * 48 * 128 * 128 * 320 * 4, 11 << 20),
        name="agg_transposed",
    )(cols, me, grad, vals)


def agg_tile(t, place, cols_ref, ext, held):
    tiles = held.shape[1]
    left = jnp.concatenate([held[place, k] for k in range(tiles)], axis=1)
    right = jnp.concatenate([ext[cols_ref[k, t]] for k in range(tiles)], axis=1)
    return dot(left, right, NT).T.astype(BF)


def agg_one_kernel(
    list_ref,
    me_ref,
    panel_ref,
    recv_ref,
    idx_ref,
    vals_ref,
    packed_ref,
    o0,
    o1,
    o2,
    o3,
    ext,
    stack,
    cols_ref,
    col_sem,
    held,
    sems,
):
    row_tiles = vals_ref.shape[0]
    lists = pltpu.make_async_copy(list_ref, cols_ref, col_sem)
    lists.start()
    for s in range(row_tiles // UNROLL):
        fetch(vals_ref, held, sems, s, UNROLL).start()
    for e in range(32):
        ext[e] = panel_ref[:, e * 128 : (e + 1) * 128]
        ext[32 + e] = unpack_pair(recv_ref[2 * e], recv_ref[2 * e + 1])
    lists.wait()

    def body(s, carry):
        fetch(vals_ref, held, sems, s, UNROLL).wait()
        for r in range(UNROLL):
            place = pl.multiple_of((s * (UNROLL // 2) + r // 2) * 32, 32)
            total = agg_tile(s * UNROLL + r, s * UNROLL + r, cols_ref, ext, held)
            stack[pl.ds(place, 32), (r % 2) * 128 : (r % 2 + 1) * 128] = total
        return carry

    lax.fori_loop(0, row_tiles // UNROLL, body, 0)
    gather_packed(stack, idx_ref, packed_ref, 32)
    me = me_ref[0]
    for d, out in enumerate((o0, o1, o2, o3)):
        for j in range(4):
            place = pl.multiple_of(((me ^ d) * 4 + j) * 32, 32)
            out[:, j * 256 : (j + 1) * 256] = stack[pl.ds(place, 32), :]


def agg_one_call(panel, received, idx, cols, vals, me):
    pieces = received.shape[0]
    out = jax.ShapeDtypeStruct((32, 1024), BF)
    return pl.pallas_call(
        agg_one_kernel,
        out_shape=(jax.ShapeDtypeStruct((pieces, 16, 128), BF),) + (out,) * 4,
        in_specs=[anywhere(), smem(), whole(), whole(), whole(), anywhere()],
        out_specs=[whole()] * 5,
        scratch_shapes=[VMEM((64, 32, 128), BF), VMEM((512, 256), BF)]
        + list_scratch(cols)
        + held_scratch(vals, UNROLL),
        compiler_params=params(LARGE),
        cost_estimate=cost(2 * 32 * 128 * 128 * 320 * 8, 11 << 20),
        name="agg_one",
    )(cols, me, panel, received, idx, vals)


def dense_body(mix, zed, w1t, w2, w2t, hid, gp, yall):
    rows = mix.shape[1]
    for c in range(rows // 256):
        lanes = slice(c * 256, (c + 1) * 256)
        pre = dot(w1t[...], mix[:, lanes])
        gate = 1.0 / (1.0 + jnp.exp(-pre))
        hidden = (pre * gate).astype(BF)
        hid[:, lanes] = hidden
        yall[:, lanes] = dot(w2t[...], hidden).astype(BF)
        gh = dot(w2[...], zed[:, lanes])
        gp[:, lanes] = (gh * gate * (1.0 + pre * (1.0 - gate))).astype(BF)
    return dot(mix[...], gp[...], NT), dot(zed[...], hid[...], NT)


def dense_own_kernel(me_ref, *refs):
    own, zs = refs[0:4], refs[4:8]
    w1t, w2, w2t = refs[8:11]
    yall, p1_ref, p2_ref = refs[11:14]
    mix, zed, hid, gp = refs[14:18]
    me = me_ref[0]
    for d in range(4):
        f = me ^ d
        mix[pl.ds(pl.multiple_of(f * 32, 32), 32), :] = own[d][...]
        zed[pl.ds(pl.multiple_of(f * 48, 16), 48), :] = zs[d][:, :1024]
    p1, p2 = dense_body(mix, zed, w1t, w2, w2t, hid, gp, yall)
    p1_ref[...] = p1
    p2_ref[...] = p2


def dense_far_kernel(me_ref, *refs):
    far, zs = refs[0:4], refs[4:8]
    w1t, w2, w2t, y_own, p1_ref, p2_ref = refs[8:14]
    ys, gs = refs[14:18], refs[18:22]
    mix, zed, hid, gp, yall, gall = refs[22:28]
    me = me_ref[0]
    for d in range(4):
        f = me ^ d
        at = pl.multiple_of(f * 32, 32)
        for e in range(8):
            pair = far[PARTNERS.index(d)]
            mix[pl.ds(at, 32), e * 128 : (e + 1) * 128] = unpack_pair(pair[2 * e], pair[2 * e + 1])
        zed[pl.ds(pl.multiple_of(f * 48, 16), 48), :] = zs[d][:, 1024:]
    p1, p2 = dense_body(mix, zed, w1t, w2, w2t, hid, gp, yall)
    for d in range(4):
        place = pl.ds(pl.multiple_of((me ^ d) * 48, 16), 48)
        ys[d][:, :1024] = y_own[place, :]
        ys[d][:, 1024:] = yall[place, :]
    p1 = p1 + p1_ref[...]
    p2 = p2 + p2_ref[...]
    gall[0:128] = p1[:, :128]
    gall[128:256] = p1[:, 128:]
    gall[256:448] = p2[:, :128]
    gall[448:640] = p2[:, 128:]
    for d in range(4):
        gs[d][...] = gall[pl.ds(pl.multiple_of((me ^ d) * 160, 8), 160), :]


def dense_scratch():
    return [
        VMEM((128, 1024), BF),
        VMEM((192, 1024), BF),
        VMEM((256, 1024), BF),
        VMEM((256, 1024), BF),
    ]


def dense_own_call(me, own, zs, w1t, w2, w2t):
    return pl.pallas_call(
        dense_own_kernel,
        out_shape=(
            jax.ShapeDtypeStruct((192, 1024), BF),
            jax.ShapeDtypeStruct((128, 256), F32),
            jax.ShapeDtypeStruct((192, 256), F32),
        ),
        in_specs=[smem()] + [whole()] * 11,
        out_specs=[whole()] * 3,
        scratch_shapes=dense_scratch(),
        compiler_params=params(),
        cost_estimate=cost(2 * 1024 * 256 * 1500, 4 << 20),
        name="dense_own",
    )(me, *own, *zs, w1t, w2, w2t)


def dense_far_call(me, far, zs, w1t, w2, w2t, y_own, p1, p2):
    return pl.pallas_call(
        dense_far_kernel,
        out_shape=(jax.ShapeDtypeStruct((48, 2048), BF),) * 4
        + (jax.ShapeDtypeStruct((160, 128), F32),) * 4,
        in_specs=[smem()] + [whole()] * 14,
        out_specs=[whole()] * 8,
        scratch_shapes=dense_scratch() + [VMEM((192, 1024), BF), VMEM((640, 128), F32)],
        compiler_params=params(),
        cost_estimate=cost(2 * 1024 * 256 * 1500, 4 << 20),
        name="dense_far",
    )(me, *far, *zs, w1t, w2, w2t, y_own, p1, p2)


def spread_kernel(me_ref, *refs):
    ext = refs[4]
    me = me_ref[0]
    for d in range(4):
        chunk = (me ^ d) * 8
        for j in range(8):
            ext[chunk + j] = refs[d][:, j * 128 : (j + 1) * 128]
            ext[32 + chunk + j] = refs[d][:, (8 + j) * 128 : (9 + j) * 128]


def spread_call(me, ys):
    return pl.pallas_call(
        spread_kernel,
        out_shape=jax.ShapeDtypeStruct((64, 48, 128), BF),
        in_specs=[smem()] + [whole()] * 4,
        out_specs=whole(),
        compiler_params=params(),
        cost_estimate=cost(0, 100 << 20),
        name="spread",
    )(me, *ys)


def agg_two_call(first, count, ext, cols, vals, classes, done):
    lead = sum(part.shape[1] for part in done)

    def kernel(cols_ref, ext_ref, vals_ref, *refs):
        out_ref = refs[-1]
        at = 0
        for part in refs[:-1]:
            out_ref[:, at : at + part.shape[1]] = part[...]
            at += part.shape[1]
        for r in range(count):
            total = agg_tile(first + r, first + r, cols_ref, ext_ref, vals_ref)
            out_ref[:, at + r * 128 : at + (r + 1) * 128] = total[:classes]

    return pl.pallas_call(
        kernel,
        out_shape=jax.ShapeDtypeStruct((classes, lead + count * 128), BF),
        in_specs=[smem()] + [whole()] * (2 + len(done)),
        out_specs=whole(),
        compiler_params=params(),
        cost_estimate=cost(2 * 48 * 128 * 128 * 10 * count * 4, count * 330000),
        name="agg_two",
    )(cols, ext, vals, *done)


def finish_kernel(me_ref, g0, g1, g2, g3, one_ref, two_ref, buf):
    me = me_ref[0]
    for d, g in zip(PARTNERS, (g0, g1, g2, g3)):
        buf[pl.ds(pl.multiple_of((me ^ d) * 160, 8), 160), :] = g[...]
    one_ref[:, :128] = buf[0:128]
    one_ref[:, 128:] = buf[128:256]
    per = two_ref.shape[0] // 4
    for f in range(4):
        two_ref[f * per : (f + 1) * per, :128] = buf[256 + 48 * f : 256 + 48 * f + per]
        two_ref[f * per : (f + 1) * per, 128:] = buf[448 + 48 * f : 448 + 48 * f + per]


def finish_call(me, gs, classes):
    return pl.pallas_call(
        finish_kernel,
        out_shape=(
            jax.ShapeDtypeStruct((128, 256), F32),
            jax.ShapeDtypeStruct((classes, 256), F32),
        ),
        in_specs=[pl.BlockSpec(memory_space=pltpu.SMEM)] + [whole()] * 4,
        out_specs=[whole()] * 2,
        scratch_shapes=[VMEM((640, 128), F32)],
        compiler_params=params(),
        name="finish",
    )(me, *gs)


def swap(x, axis, size, mask):
    return lax.ppermute(x, axis, [(i, i ^ mask) for i in range(size)])


def after(x, *others):
    return lax.optimization_barrier((x, *others))[0]


def on_device(
    features, weight_one, weight_two, grad_logits, send_idx, send_count, tile_cols, tile_vals
):
    partitions = lax.axis_size("dom")
    feat = lax.axis_size("feat")
    me = lax.axis_index("feat").astype(jnp.int32)
    me_arr = me.reshape(1)
    class_cols = grad_logits.shape[1]
    hidden = weight_one.shape[1]

    def swap_feat(x, d):
        return swap(x, "feat", feat, d)

    def swap_dom(x, mask):
        return swap(x, "dom", partitions, mask)

    panel = features.T
    grad = grad_logits.T
    cols = tile_cols.T
    w2 = jnp.pad(weight_two.reshape(hidden, feat, class_cols), ((0, 0), (0, 0), (0, 48 - class_cols)))
    w2 = w2.reshape(hidden, feat * 48)
    w1t = weight_one.T
    w2t = w2.T

    packed_one, idx = gather_call(panel, send_idx, send_count)
    received_one = lax.all_to_all(packed_one, "dom", split_axis=0, concat_axis=0, tiled=True)
    zs = transpose_agg_call(grad, cols, tile_vals, me_arr)
    received_one = after(received_one, zs[0])
    zs = [zs[0]] + [swap_feat(zs[d], d) for d in (1, 2, 3)]
    packed_two, *mixed = agg_one_call(panel, received_one, idx, cols, tile_vals, me_arr)
    packed_two = after(packed_two, zs[1], zs[3])
    received_two = lax.all_to_all(packed_two, "dom", split_axis=0, concat_axis=0, tiled=True)
    own = [mixed[0]] + [swap_feat(mixed[d], d) for d in (1, 2, 3)]
    pieces = partitions // feat

    def far_block(d):
        return lax.dynamic_slice_in_dim(received_two, (me ^ d) * pieces, pieces, 0)

    near = far_block(0)
    far = [near] + [swap_feat(far_block(d), d) for d in PARTNERS[1:]]
    own[0] = after(own[0], near)
    y_own, p1, p2 = dense_own_call(me_arr, own, zs, w1t, w2, w2t)
    outs = dense_far_call(me_arr, far, zs, w1t, w2, w2t, y_own, p1, p2)
    ys, gs = outs[:4], outs[4:]
    moved = [swap_feat(gs[d], d) for d in (1, 2, 3)]
    total = (moved[1] + moved[2]) + (gs[0] + moved[0])
    ys = [ys[0]] + [swap_feat(ys[d], d) for d in (1, 2, 3)]
    total = total + swap_dom(total, 1)
    moved = [swap_dom(total, 16 * d) for d in (1, 2, 3)]
    total = (total + moved[0]) + (moved[2] + moved[1])
    ext = spread_call(me_arr, ys)
    out = []
    row_tiles = tile_cols.shape[0]
    cuts = [0, row_tiles // 16, row_tiles * 21 // 32, row_tiles]

    def beside(moved):
        first, last = cuts[len(out) : len(out) + 2]
        done = out if last == row_tiles else []
        out.append(agg_two_call(first, last - first, ext, cols, tile_vals, class_cols, done))
        *moved, out[-1] = lax.optimization_barrier((*moved, out[-1]))
        return moved

    ext, total = lax.optimization_barrier((ext, total))
    (moved,) = beside([swap_dom(total, 8)])
    total = total + moved
    ext, total = lax.optimization_barrier((ext, total))
    moved = beside([swap_dom(total, d) for d in (2, 4, 6)])
    total = (total + moved[0]) + (moved[2] + moved[1])
    ext, total = lax.optimization_barrier((ext, total))
    moved = beside([swap_feat(total, d) for d in PARTNERS[1:]])
    logits = out[-1]
    grad_one, grad_two = finish_call(me_arr, [total] + moved, feat * class_cols)
    return (logits.T, grad_one, grad_two.T)


def solution(mesh):
    return jax.shard_map(
        on_device,
        mesh=mesh,
        in_specs=(
            P("dom", "feat"),
            P(),
            P(),
            P("dom", "feat"),
            P("dom", None),
            P("dom"),
            P("dom", None),
            P("dom", None, None, None),
        ),
        out_specs=(P("dom", "feat"), P(), P()),
        check_vma=False,
    )
```

```python
import functools

import jax
import jax.numpy as jnp
from jax import lax
from jax.experimental import pallas as pl
from jax.experimental.pallas import tpu as pltpu
from jax.sharding import PartitionSpec as P

BF = jnp.bfloat16
F32 = jnp.float32
VMEM = pltpu.VMEM
LIMIT = 24 * 1024 * 1024
LARGE = 48 * 1024 * 1024
PARTNERS = (0, 1, 3, 2)
NT = (((1,), (1,)), ((), ()))
NN = (((1,), (0,)), ((), ()))


def dot(a, b, dims=NN):
    return lax.dot_general(a, b, dims, preferred_element_type=F32)


def params(limit=LIMIT):
    return pltpu.CompilerParams(vmem_limit_bytes=limit)


def cost(flops, nbytes):
    return pl.CostEstimate(flops=flops, bytes_accessed=nbytes, transcendentals=0)


def whole():
    return pl.BlockSpec(memory_space=VMEM)


def gather_packed(stack_ref, idx_ref, out_ref, cols):
    chunks = stack_ref.shape[0] // cols
    lanes = stack_ref.shape[1]
    row_ids = lax.broadcasted_iota(jnp.int32, (lanes, 256), 0)
    low = lax.broadcasted_iota(jnp.int32, (16, 128), 1) < 64

    def step(j, carry):
        idx = idx_ref[pl.ds(j, 1), :]
        hot = (row_ids == (idx & (lanes - 1))).astype(BF)
        part = idx >> (lanes.bit_length() - 1)
        got = jnp.zeros((cols, 256), F32)
        wide = dot(stack_ref[...], hot)
        for c in range(chunks):
            got = jnp.where(part == c, wide[c * cols : (c + 1) * cols], got)
        for pair in range(2):
            top = got[:16, pair * 128 : (pair + 1) * 128]
            bottom = got[16:, pair * 128 : (pair + 1) * 128]
            first = jnp.where(low, top, pltpu.roll(bottom, 64, 1))
            second = jnp.where(low, pltpu.roll(top, 64, 1), bottom)
            out_ref[j * 4 + pair * 2] = first.astype(BF)
            out_ref[j * 4 + pair * 2 + 1] = second.astype(BF)
        return carry

    lax.fori_loop(0, idx_ref.shape[0], step, 0, unroll=16)


def unpack_pair(first, second):
    low = lax.broadcasted_iota(jnp.int32, (16, 128), 1) < 64
    first, second = first.astype(F32), second.astype(F32)
    top = jnp.where(low, first, pltpu.roll(second, 64, 1))
    bottom = jnp.where(low, pltpu.roll(first, 64, 1), second)
    return jnp.concatenate([top, bottom], axis=0).astype(BF)


def gather_kernel(live_ref, panel_ref, send_ref, out_ref, idx_ref, stack_ref, lists, count_ref, sems):
    cols = panel_ref.shape[0]
    lanes = stack_ref.shape[1]
    chunks = panel_ref.shape[1] // lanes
    copies = [
        pltpu.make_async_copy(live_ref, count_ref, sems.at[chunks + 1]),
        pltpu.make_async_copy(send_ref, lists, sems.at[chunks]),
    ] + [
        pltpu.make_async_copy(
            panel_ref.at[:, pl.ds(c * lanes, lanes)], stack_ref.at[pl.ds(c * cols, cols), :], sems.at[c]
        )
        for c in range(chunks)
    ]
    for copy in copies:
        copy.start()
    copies[0].wait()
    copies[1].wait()
    bound = lists.shape[1]
    slot = lax.broadcasted_iota(jnp.int32, (1, bound), 1)
    per = lanes // bound
    for j in range(idx_ref.shape[0]):
        rows = [
            jnp.where(slot < count_ref[q], lists[q : q + 1, :], -1) for q in range(j * per, (j + 1) * per)
        ]
        idx_ref[j : j + 1, :] = jnp.concatenate(rows, axis=1)
    for copy in copies[2:]:
        copy.wait()
    gather_packed(stack_ref, idx_ref, out_ref, cols)


def gather_call(panel, send_idx, send_count):
    cols, rows = panel.shape
    pieces, bound = send_idx.shape
    return pl.pallas_call(
        gather_kernel,
        out_shape=(
            jax.ShapeDtypeStruct((pieces, 16, 128), BF),
            jax.ShapeDtypeStruct((pieces * bound // 256, 256), jnp.int32),
        ),
        in_specs=[anywhere()] * 3,
        out_specs=[whole(), whole()],
        scratch_shapes=[
            VMEM((rows // 256 * cols, 256), BF),
            VMEM((pieces, bound), jnp.int32),
            pltpu.SMEM((pieces,), jnp.int32),
            pltpu.SemaphoreType.DMA((rows // 256 + 2,)),
        ],
        compiler_params=params(60 * 1024 * 1024),
        cost_estimate=cost(2 * 512 * 256 * 4096, 1 << 20),
        name="gather_rows",
    )(send_count, panel, send_idx)


def smem():
    return pl.BlockSpec(memory_space=pltpu.SMEM)


UNROLL = 8


def anywhere():
    return pl.BlockSpec(memory_space=pl.ANY)


def held_scratch(vals, group):
    return [VMEM(vals.shape, vals.dtype), pltpu.SemaphoreType.DMA((vals.shape[0] // group,))]


def list_scratch(cols):
    return [pltpu.SMEM(cols.shape, cols.dtype), pltpu.SemaphoreType.DMA]


def fetch(vals_ref, held, sems, s, group, first=0):
    return pltpu.make_async_copy(
        vals_ref.at[pl.ds(first + s * group, group)], held.at[pl.ds(s * group, group)], sems.at[s]
    )


def transpose_agg_kernel(list_ref, me_ref, grad_ref, vals_ref, o0, o1, o2, o3, acc, cols_ref, col_sem, held, sems):
    row_tiles, tiles = vals_ref.shape[:2]
    classes = grad_ref.shape[0]
    lists = pltpu.make_async_copy(list_ref, cols_ref, col_sem)
    lists.start()
    for s in range(row_tiles // UNROLL):
        fetch(vals_ref, held, sems, s, UNROLL).start()
    acc[...] = jnp.zeros_like(acc)
    lists.wait()

    def body(s, carry):
        fetch(vals_ref, held, sems, s, UNROLL).wait()
        for r in range(UNROLL):
            t = s * UNROLL + r
            slab = grad_ref[:, pl.ds(pl.multiple_of(t * 128, 128), 128)]
            side = jnp.concatenate([held[t, k] for k in range(tiles)], axis=1)
            part = dot(slab, side)
            for k in range(tiles):
                acc[cols_ref[k, t], :classes] += part[:, k * 128 : (k + 1) * 128]
        return carry

    lax.fori_loop(0, row_tiles // UNROLL, body, 0)
    me = me_ref[0]
    for d, out in enumerate((o0, o1, o2, o3)):
        chunk = (me ^ d) * 8
        for j in range(8):
            out[:, j * 128 : (j + 1) * 128] = acc[chunk + j].astype(BF)
            out[:, (8 + j) * 128 : (9 + j) * 128] = acc[32 + chunk + j].astype(BF)


def transpose_agg_call(grad, cols, vals, me):
    width = 48
    return pl.pallas_call(
        transpose_agg_kernel,
        out_shape=(jax.ShapeDtypeStruct((width, 2048), BF),) * 4,
        in_specs=[anywhere(), smem(), whole(), anywhere()],
        out_specs=[whole()] * 4,
        scratch_shapes=[VMEM((64, width, 128), F32)] + list_scratch(cols) + held_scratch(vals, UNROLL),
        compiler_params=params(LARGE),
        cost_estimate=cost(2 * 48 * 128 * 128 * 320 * 4, 11 << 20),
        name="agg_transposed",
    )(cols, me, grad, vals)


def agg_tile(t, place, cols_ref, ext, held):
    tiles = held.shape[1]
    left = jnp.concatenate([held[place, k] for k in range(tiles)], axis=1)
    right = jnp.concatenate([ext[cols_ref[k, t]] for k in range(tiles)], axis=1)
    return dot(left, right, NT).T.astype(BF)


def agg_one_kernel(
    list_ref,
    me_ref,
    panel_ref,
    recv_ref,
    idx_ref,
    vals_ref,
    packed_ref,
    o0,
    o1,
    o2,
    o3,
    ext,
    stack,
    cols_ref,
    col_sem,
    held,
    sems,
):
    row_tiles = vals_ref.shape[0]
    lists = pltpu.make_async_copy(list_ref, cols_ref, col_sem)
    lists.start()
    for s in range(row_tiles // UNROLL):
        fetch(vals_ref, held, sems, s, UNROLL).start()
    for e in range(32):
        ext[e] = panel_ref[:, e * 128 : (e + 1) * 128]
        ext[32 + e] = unpack_pair(recv_ref[2 * e], recv_ref[2 * e + 1])
    lists.wait()

    def body(s, carry):
        fetch(vals_ref, held, sems, s, UNROLL).wait()
        for r in range(UNROLL):
            place = pl.multiple_of((s * (UNROLL // 2) + r // 2) * 32, 32)
            total = agg_tile(s * UNROLL + r, s * UNROLL + r, cols_ref, ext, held)
            stack[pl.ds(place, 32), (r % 2) * 128 : (r % 2 + 1) * 128] = total
        return carry

    lax.fori_loop(0, row_tiles // UNROLL, body, 0)
    gather_packed(stack, idx_ref, packed_ref, 32)
    me = me_ref[0]
    for d, out in enumerate((o0, o1, o2, o3)):
        for j in range(4):
            place = pl.multiple_of(((me ^ d) * 4 + j) * 32, 32)
            out[:, j * 256 : (j + 1) * 256] = stack[pl.ds(place, 32), :]


def agg_one_call(panel, received, idx, cols, vals, me):
    pieces = received.shape[0]
    out = jax.ShapeDtypeStruct((32, 1024), BF)
    return pl.pallas_call(
        agg_one_kernel,
        out_shape=(jax.ShapeDtypeStruct((pieces, 16, 128), BF),) + (out,) * 4,
        in_specs=[anywhere(), smem(), whole(), whole(), whole(), anywhere()],
        out_specs=[whole()] * 5,
        scratch_shapes=[VMEM((64, 32, 128), BF), VMEM((512, 256), BF)]
        + list_scratch(cols)
        + held_scratch(vals, UNROLL),
        compiler_params=params(LARGE),
        cost_estimate=cost(2 * 32 * 128 * 128 * 320 * 8, 11 << 20),
        name="agg_one",
    )(cols, me, panel, received, idx, vals)


def dense_body(mix, zed, w1t, w2, w2t, hid, gp, yall):
    rows = mix.shape[1]
    for c in range(rows // 256):
        lanes = slice(c * 256, (c + 1) * 256)
        pre = dot(w1t[...], mix[:, lanes])
        gate = 1.0 / (1.0 + jnp.exp(-pre))
        hidden = (pre * gate).astype(BF)
        hid[:, lanes] = hidden
        yall[:, lanes] = dot(w2t[...], hidden).astype(BF)
        gh = dot(w2[...], zed[:, lanes])
        gp[:, lanes] = (gh * gate * (1.0 + pre * (1.0 - gate))).astype(BF)
    return dot(mix[...], gp[...], NT), dot(zed[...], hid[...], NT)


def dense_own_kernel(me_ref, *refs):
    own, zs = refs[0:4], refs[4:8]
    w1t, w2, w2t = refs[8:11]
    yall, p1_ref, p2_ref = refs[11:14]
    mix, zed, hid, gp = refs[14:18]
    me = me_ref[0]
    for d in range(4):
        f = me ^ d
        mix[pl.ds(pl.multiple_of(f * 32, 32), 32), :] = own[d][...]
        zed[pl.ds(pl.multiple_of(f * 48, 16), 48), :] = zs[d][:, :1024]
    p1, p2 = dense_body(mix, zed, w1t, w2, w2t, hid, gp, yall)
    p1_ref[...] = p1
    p2_ref[...] = p2


def dense_far_kernel(me_ref, *refs):
    far, zs = refs[0:4], refs[4:8]
    w1t, w2, w2t, y_own, p1_ref, p2_ref = refs[8:14]
    ys, gs = refs[14:18], refs[18:22]
    mix, zed, hid, gp, yall, gall = refs[22:28]
    me = me_ref[0]
    for d in range(4):
        f = me ^ d
        at = pl.multiple_of(f * 32, 32)
        for e in range(8):
            pair = far[PARTNERS.index(d)]
            mix[pl.ds(at, 32), e * 128 : (e + 1) * 128] = unpack_pair(pair[2 * e], pair[2 * e + 1])
        zed[pl.ds(pl.multiple_of(f * 48, 16), 48), :] = zs[d][:, 1024:]
    p1, p2 = dense_body(mix, zed, w1t, w2, w2t, hid, gp, yall)
    for d in range(4):
        place = pl.ds(pl.multiple_of((me ^ d) * 48, 16), 48)
        ys[d][:, :1024] = y_own[place, :]
        ys[d][:, 1024:] = yall[place, :]
    p1 = p1 + p1_ref[...]
    p2 = p2 + p2_ref[...]
    gall[0:128] = p1[:, :128]
    gall[128:256] = p1[:, 128:]
    gall[256:448] = p2[:, :128]
    gall[448:640] = p2[:, 128:]
    for d in range(4):
        gs[d][...] = gall[pl.ds(pl.multiple_of((me ^ d) * 160, 8), 160), :]


def dense_scratch():
    return [
        VMEM((128, 1024), BF),
        VMEM((192, 1024), BF),
        VMEM((256, 1024), BF),
        VMEM((256, 1024), BF),
    ]


def dense_own_call(me, own, zs, w1t, w2, w2t):
    return pl.pallas_call(
        dense_own_kernel,
        out_shape=(
            jax.ShapeDtypeStruct((192, 1024), BF),
            jax.ShapeDtypeStruct((128, 256), F32),
            jax.ShapeDtypeStruct((192, 256), F32),
        ),
        in_specs=[smem()] + [whole()] * 11,
        out_specs=[whole()] * 3,
        scratch_shapes=dense_scratch(),
        compiler_params=params(),
        cost_estimate=cost(2 * 1024 * 256 * 1500, 4 << 20),
        name="dense_own",
    )(me, *own, *zs, w1t, w2, w2t)


def dense_far_call(me, far, zs, w1t, w2, w2t, y_own, p1, p2):
    return pl.pallas_call(
        dense_far_kernel,
        out_shape=(jax.ShapeDtypeStruct((48, 2048), BF),) * 4
        + (jax.ShapeDtypeStruct((160, 128), F32),) * 4,
        in_specs=[smem()] + [whole()] * 14,
        out_specs=[whole()] * 8,
        scratch_shapes=dense_scratch() + [VMEM((192, 1024), BF), VMEM((640, 128), F32)],
        compiler_params=params(),
        cost_estimate=cost(2 * 1024 * 256 * 1500, 4 << 20),
        name="dense_far",
    )(me, *far, *zs, w1t, w2, w2t, y_own, p1, p2)


def spread_kernel(me_ref, *refs):
    ext = refs[4]
    me = me_ref[0]
    for d in range(4):
        chunk = (me ^ d) * 8
        for j in range(8):
            ext[chunk + j] = refs[d][:, j * 128 : (j + 1) * 128]
            ext[32 + chunk + j] = refs[d][:, (8 + j) * 128 : (9 + j) * 128]


def spread_call(me, ys):
    return pl.pallas_call(
        spread_kernel,
        out_shape=jax.ShapeDtypeStruct((64, 48, 128), BF),
        in_specs=[smem()] + [whole()] * 4,
        out_specs=whole(),
        compiler_params=params(),
        cost_estimate=cost(0, 100 << 20),
        name="spread",
    )(me, *ys)


def agg_two_call(first, count, ext, cols, vals, classes, done):
    lead = sum(part.shape[1] for part in done)

    def kernel(cols_ref, ext_ref, vals_ref, *refs):
        out_ref = refs[-1]
        at = 0
        for part in refs[:-1]:
            out_ref[:, at : at + part.shape[1]] = part[...]
            at += part.shape[1]
        for r in range(count):
            total = agg_tile(first + r, first + r, cols_ref, ext_ref, vals_ref)
            out_ref[:, at + r * 128 : at + (r + 1) * 128] = total[:classes]

    return pl.pallas_call(
        kernel,
        out_shape=jax.ShapeDtypeStruct((classes, lead + count * 128), BF),
        in_specs=[smem()] + [whole()] * (2 + len(done)),
        out_specs=whole(),
        compiler_params=params(),
        cost_estimate=cost(2 * 48 * 128 * 128 * 10 * count * 4, count * 330000),
        name="agg_two",
    )(cols, ext, vals, *done)


def finish_kernel(me_ref, g0, g1, g2, g3, one_ref, two_ref, buf):
    me = me_ref[0]
    for d, g in zip(PARTNERS, (g0, g1, g2, g3)):
        buf[pl.ds(pl.multiple_of((me ^ d) * 160, 8), 160), :] = g[...]
    one_ref[:, :128] = buf[0:128]
    one_ref[:, 128:] = buf[128:256]
    per = two_ref.shape[0] // 4
    for f in range(4):
        two_ref[f * per : (f + 1) * per, :128] = buf[256 + 48 * f : 256 + 48 * f + per]
        two_ref[f * per : (f + 1) * per, 128:] = buf[448 + 48 * f : 448 + 48 * f + per]


def finish_call(me, gs, classes):
    return pl.pallas_call(
        finish_kernel,
        out_shape=(
            jax.ShapeDtypeStruct((128, 256), F32),
            jax.ShapeDtypeStruct((classes, 256), F32),
        ),
        in_specs=[pl.BlockSpec(memory_space=pltpu.SMEM)] + [whole()] * 4,
        out_specs=[whole()] * 2,
        scratch_shapes=[VMEM((640, 128), F32)],
        compiler_params=params(),
        name="finish",
    )(me, *gs)


def swap(x, axis, size, mask):
    return lax.ppermute(x, axis, [(i, i ^ mask) for i in range(size)])


def after(x, *others):
    return lax.optimization_barrier((x, *others))[0]


def on_device(
    features, weight_one, weight_two, grad_logits, send_idx, send_count, tile_cols, tile_vals
):
    partitions = lax.axis_size("dom")
    feat = lax.axis_size("feat")
    me = lax.axis_index("feat").astype(jnp.int32)
    me_arr = me.reshape(1)
    class_cols = grad_logits.shape[1]
    hidden = weight_one.shape[1]

    def swap_feat(x, d):
        return swap(x, "feat", feat, d)

    def swap_dom(x, mask):
        return swap(x, "dom", partitions, mask)

    panel = features.T
    grad = grad_logits.T
    cols = tile_cols.T
    w2 = jnp.pad(weight_two.reshape(hidden, feat, class_cols), ((0, 0), (0, 0), (0, 48 - class_cols)))
    w2 = w2.reshape(hidden, feat * 48)
    w1t = weight_one.T
    w2t = w2.T

    packed_one, idx = gather_call(panel, send_idx, send_count)
    received_one = lax.all_to_all(packed_one, "dom", split_axis=0, concat_axis=0, tiled=True)
    zs = transpose_agg_call(grad, cols, tile_vals, me_arr)
    received_one = after(received_one, zs[0])
    zs = [zs[0]] + [swap_feat(zs[d], d) for d in (1, 2, 3)]
    packed_two, *mixed = agg_one_call(panel, received_one, idx, cols, tile_vals, me_arr)
    packed_two = after(packed_two, zs[1], zs[3])
    received_two = lax.all_to_all(packed_two, "dom", split_axis=0, concat_axis=0, tiled=True)
    own = [mixed[0]] + [swap_feat(mixed[d], d) for d in (1, 2, 3)]
    pieces = partitions // feat

    def far_block(d):
        return lax.dynamic_slice_in_dim(received_two, (me ^ d) * pieces, pieces, 0)

    near = far_block(0)
    far = [near] + [swap_feat(far_block(d), d) for d in PARTNERS[1:]]
    own[0] = after(own[0], near)
    y_own, p1, p2 = dense_own_call(me_arr, own, zs, w1t, w2, w2t)
    outs = dense_far_call(me_arr, far, zs, w1t, w2, w2t, y_own, p1, p2)
    ys, gs = outs[:4], outs[4:]
    moved = [swap_feat(gs[d], d) for d in (1, 2, 3)]
    total = (moved[1] + moved[2]) + (gs[0] + moved[0])
    ys = [ys[0]] + [swap_feat(ys[d], d) for d in (1, 2, 3)]
    total = total + swap_dom(total, 1)
    moved = [swap_dom(total, 16 * d) for d in (1, 2, 3)]
    total = (total + moved[0]) + (moved[2] + moved[1])
    ext = spread_call(me_arr, ys)
    out = []
    row_tiles = tile_cols.shape[0]
    cuts = [0, row_tiles // 16, row_tiles * 23 // 32, row_tiles]

    def beside(moved):
        first, last = cuts[len(out) : len(out) + 2]
        done = out if last == row_tiles else []
        out.append(agg_two_call(first, last - first, ext, cols, tile_vals, class_cols, done))
        *moved, out[-1] = lax.optimization_barrier((*moved, out[-1]))
        return moved

    ext, total = lax.optimization_barrier((ext, total))
    (moved,) = beside([swap_dom(total, 8)])
    total = total + moved
    ext, total = lax.optimization_barrier((ext, total))
    moved = beside([swap_dom(total, d) for d in (2, 4, 6)])
    total = (total + moved[0]) + (moved[2] + moved[1])
    ext, total = lax.optimization_barrier((ext, total))
    moved = beside([swap_feat(total, d) for d in PARTNERS[1:]])
    logits = out[-1]
    grad_one, grad_two = finish_call(me_arr, [total] + moved, feat * class_cols)
    return (logits.T, grad_one, grad_two.T)


def solution(mesh):
    return jax.shard_map(
        on_device,
        mesh=mesh,
        in_specs=(
            P("dom", "feat"),
            P(),
            P(),
            P("dom", "feat"),
            P("dom", None),
            P("dom"),
            P("dom", None),
            P("dom", None, None, None),
        ),
        out_specs=(P("dom", "feat"), P(), P()),
        check_vma=False,
    )
```
